32 devices in a mesh: dp: 8 (over y, x, core), tensor: 4 (over z).
Axes of the slice: x: 2, y: 2, z: 4, core: 2. Of those that a mesh axis runs over, the one named last changes fastest.
Arguments:
- block_in: bfloat16 [4096, 768], P(('dp', 'tensor')), may hold values from -6 to 6
- segment_ids: int32 [8, 512], P('dp'), may hold values from 0 to 3, never falling along the last dimension, each value on 1 to 384 neighbouring positions
- first_norm_gain: float32 [768], replicated, may hold values from 0.5 to 1.5
- first_norm_bias: float32 [768], replicated, may hold values from -3 to 3
- qkv_weight: bfloat16 [768, 3, 768], P(None, None, 'tensor'), may hold values from -1 to 1
- qv_bias: float32 [2, 768], P(None, 'tensor'), may hold values from -3 to 3
- out_weight: bfloat16 [768, 768], P('tensor'), may hold values from -0.875 to 0.875
- out_bias: float32 [768], replicated, may hold values from -3 to 3
- second_norm_gain: float32 [768], replicated, may hold values from 0.5 to 1.5
- second_norm_bias: float32 [768], replicated, may hold values from -3 to 3
- fc_weight: bfloat16 [768, 3072], P(None, 'tensor'), may hold values from -0.21875 to 0.21875
- fc_bias: float32 [3072], P('tensor'), may hold values from -3 to 3
- proj_weight: bfloat16 [3072, 768], P('tensor'), may hold values from -0.109375 to 0.109375
- proj_bias: float32 [768], replicated, may hold values from -3 to 3
- out_grad: bfloat16 [4096, 768], P(('dp', 'tensor')), may hold values from -6 to 6
Outputs:
- block_out: float32 [4096, 768], P(('dp', 'tensor'))
- d_in: float32 [4096, 768], P(('dp', 'tensor'))
- d_ln1_gain: float32 [768], replicated
- d_ln1_bias: float32 [768], replicated
- d_qkv_weight: float32 [768, 3, 768], P(None, None, 'tensor')
- d_qv_bias: float32 [2, 768], P(None, 'tensor')
- d_out_weight: float32 [768, 768], P('tensor')
- d_out_bias: float32 [768], replicated
- d_ln2_gain: float32 [768], replicated
- d_ln2_bias: float32 [768], replicated
- d_fc_weight: float32 [768, 3072], P(None, 'tensor')
- d_fc_bias: float32 [3072], P('tensor')
- d_proj_weight: float32 [3072, 768], P('tensor')
- d_proj_bias: float32 [768], replicated
The draws below stay inside these ranges and needn't reach their ends.
Inputs may be any that keep to these rules, and one draw needn't show every extreme that they name: `segment_ids`: within each row of 512 tokens the numbers never fall.
All inputs are finite; a program needn't handle non-finite values.
Results may differ from the reference program's by a relative error of at most 0.012.
Values may be sent and summed in bfloat16 or wider, within the bound.
A program may use at most 64 MiB of HBM per device.

```python
import math
import jax
import jax.numpy as jnp
import numpy as np
from jax import lax

D = 768
HEADS = 12
HD = 64
FF = 3072
SEQ_LEN = 512
SEQS = 8
TOKENS = 4096


def draw_block_in(key, part):
    jitter = jax.random.normal(jax.random.fold_in(key, 2), (TOKENS, D), jnp.float32)
    values = jnp.clip(jitter, -6.0, 6.0)
    return values.astype(jnp.bfloat16)


def draw_qkv_weight(key, part):
    normal_part = jax.random.normal(jax.random.fold_in(key, 3), (D, 3, D), jnp.float32)
    values = jnp.clip(normal_part, -4.0, 4.0) * (1.0 / math.sqrt(D))
    return values.astype(jnp.bfloat16)


def block_scale(own_key, extent, split, least, largest):
    def one(axis_at, shards_of):
        steps = jax.random.uniform(jax.random.fold_in(jax.random.fold_in(own_key, 6), axis_at), (shards_of,), jnp.float32, least / len(split), largest / len(split))
        return jnp.repeat(jnp.exp(steps), extent[axis_at] // shards_of).reshape((-1,) + (1,) * (len(extent) - axis_at - 1))

    factor_of = one(*split[0])
    for cut in split[1:]:
        factor_of = factor_of * one(*cut)
    return factor_of


def length_profile(amount, total, limit, slope):
    portions = [(1 << 20) // math.isqrt(grade ** slope) + 1 for grade in range(2, amount + 1)]
    rest, holding = total - limit - (amount - 1), [1] * (amount - 1)
    while rest > 0:
        free = [i for i in range(amount - 1) if holding[i] < limit]
        mass, remaining = sum([portions[i] for i in free]), rest
        for i in free:
            extra = min(limit - holding[i], max(1, remaining * portions[i] // mass), rest)
            holding[i] = holding[i] + extra
            rest = rest - extra
    return np.array([limit] + holding)


def uneven(stream_key, amount, total, most, skew):
    if amount == 2:
        one = jax.random.randint(stream_key, (), max(1, total - most), min(most, total - 1) + 1)
        return jnp.stack([one, total - one])
    sizes = jnp.asarray(length_profile(amount, total, most, skew), jnp.int32)
    couples = (amount - 1) // 2
    giver, taker = sizes[1:1 + 2 * couples:2], sizes[2:2 + 2 * couples:2]
    slack = jnp.minimum(giver - 1, most - taker)
    moved = jax.random.randint(jax.random.fold_in(stream_key, 1), (couples,), 0, 1 << 20) % (slack + 1)
    sizes = sizes.at[1:1 + 2 * couples:2].set(giver - moved).at[2:2 + 2 * couples:2].set(taker + moved)
    return sizes[jax.random.permutation(jax.random.fold_in(stream_key, 2), amount)]


def gaussian(own_key, shape, spread, limit, shards=(), kind=jnp.bfloat16):
    gain = block_scale(own_key, shape, shards, -0.22, 0.18) if shards else 1.0
    array = jax.random.normal(own_key, shape, jnp.float32) * spread * gain
    return jnp.minimum(jnp.maximum(array, -limit), limit).astype(kind)


def setup_inputs(seed: int = 0) -> dict:
    arg_keys = jax.random.split(jax.random.key(seed), 16)
    return {
        "block_in": draw_block_in(jax.random.fold_in(arg_keys[15], 71), 0),
        "segment_ids": jax.vmap(lambda own: jnp.searchsorted(jnp.cumsum(uneven(own, 4, SEQ_LEN, 3 * SEQ_LEN // 4, 0)), jnp.arange(SEQ_LEN), side="right"))(jax.random.split(arg_keys[1], SEQS)).reshape((SEQS, SEQ_LEN)).astype(jnp.int32),
        "first_norm_gain": jnp.clip(1.0 + 0.1 * jax.random.normal(arg_keys[2], (D,), jnp.float32), 0.5, 1.5),
        "first_norm_bias": gaussian(arg_keys[3], (D,), 0.5, 3.0, (), jnp.float32),
        "qkv_weight": draw_qkv_weight(jax.random.fold_in(arg_keys[15], 71), 0),
        "qv_bias": gaussian(arg_keys[5], (2, D), 0.5, 3.0, ((1, 4),), jnp.float32),
        "out_weight": gaussian(arg_keys[6], (D, D), (D // 16) ** -0.5, 0.875, ((0, 4),)),
        "out_bias": gaussian(arg_keys[7], (D,), 0.5, 3.0, (), jnp.float32),
        "second_norm_gain": jnp.clip(1.0 + 0.1 * jax.random.normal(arg_keys[8], (D,), jnp.float32), 0.5, 1.5),
        "second_norm_bias": gaussian(arg_keys[9], (D,), 0.5, 3.0, (), jnp.float32),
        "fc_weight": gaussian(arg_keys[10], (D, FF), D ** -0.5, 0.21875, ((1, 4),)),
        "fc_bias": gaussian(arg_keys[11], (FF,), 0.5, 3.0, ((0, 4),), jnp.float32),
        "proj_weight": gaussian(arg_keys[12], (FF, D), FF ** -0.5, 0.109375, ((0, 4),)),
        "proj_bias": gaussian(arg_keys[13], (D,), 0.5, 3.0, (), jnp.float32),
        "out_grad": gaussian(arg_keys[14], (TOKENS, D), 1.0, 6.0, ((0, 32),)),
    }


EPS = 1e-05
GELU_C = math.sqrt(2.0 / math.pi)

def apply_layer_norm(values, scale_gain, shift_bias):
    centered_input = values - lax.optimization_barrier(jnp.mean(values, axis=-1, keepdims=True))
    variance = lax.optimization_barrier(jnp.mean(centered_input * centered_input, axis=-1, keepdims=True))
    inverse_deviation = lax.rsqrt(variance + EPS)
    normalized_input = centered_input * inverse_deviation
    return (normalized_input * scale_gain + shift_bias, normalized_input, inverse_deviation)

def layer_norm_backward(upstream_gradient, normalized_input, inverse_deviation, scale_gain):
    scaled_gradient = upstream_gradient * scale_gain
    incoming_gradient = inverse_deviation * (scaled_gradient - lax.optimization_barrier(jnp.mean(scaled_gradient, axis=-1, keepdims=True)) - normalized_input * lax.optimization_barrier(jnp.mean(scaled_gradient * normalized_input, axis=-1, keepdims=True)))
    return (incoming_gradient, lax.optimization_barrier(jnp.sum(upstream_gradient * normalized_input, axis=0)), lax.optimization_barrier(jnp.sum(upstream_gradient, axis=0)))

def gelu(value):
    return 0.5 * value * (1.0 + jnp.tanh(GELU_C * (value + 0.044715 * value ** 3)))

def gelu_grad(value):
    tangent = jnp.tanh(GELU_C * (value + 0.044715 * value ** 3))
    return 0.5 * (1.0 + tangent) + 0.5 * value * (1.0 - tangent * tangent) * GELU_C * (1.0 + 3.0 * 0.044715 * value * value)

def probs(query, key, segs):
    length = segs.shape[0]
    scores = jnp.einsum('qhd,khd->hqk', query.astype(jnp.float32), key.astype(jnp.float32)) * 0.125
    rows = jnp.arange(length)
    allowed = (segs[:, None] == segs[None, :]) & (rows[:, None] >= rows[None, :])
    return jnp.where(allowed[None], scores, -1e+30)

def attend(query, key, value, segs):
    scores = probs(query, key, segs)
    top = lax.optimization_barrier(jnp.max(scores, axis=-1, keepdims=True))
    lse = top[..., 0] + jnp.log(lax.optimization_barrier(jnp.sum(jnp.exp(scores - top), axis=-1)))
    weights = jnp.exp(scores - lse[..., None]).astype(jnp.bfloat16)
    output = jnp.einsum('hqk,khd->qhd', weights.astype(jnp.float32), value.astype(jnp.float32))
    return (output.astype(jnp.bfloat16), lse)

def attend_back(query, key, value, segs, output, lse, d_out):
    weights = jnp.exp(probs(query, key, segs) - lse[..., None])
    rounded = weights.astype(jnp.bfloat16).astype(jnp.float32)
    d_outf = d_out.astype(jnp.float32)
    d_value = jnp.einsum('hqk,qhd->khd', rounded, d_outf)
    d_probs = jnp.einsum('qhd,khd->hqk', d_outf, value.astype(jnp.float32))
    delta = jnp.transpose(lax.optimization_barrier(jnp.sum(d_outf * output.astype(jnp.float32), axis=-1)))
    d_scores = (weights * (d_probs - delta[..., None]) * 0.125).astype(jnp.bfloat16).astype(jnp.float32)
    d_query = jnp.einsum('hqk,khd->qhd', d_scores, key.astype(jnp.float32))
    d_key = jnp.einsum('hqk,qhd->khd', d_scores, query.astype(jnp.float32))
    return (d_query.astype(jnp.bfloat16), d_key.astype(jnp.bfloat16), d_value.astype(jnp.bfloat16))

def reference(block_in, segment_ids, first_norm_gain, first_norm_bias, qkv_weight, qv_bias, out_weight, out_bias, second_norm_gain, second_norm_bias, fc_weight, fc_bias, proj_weight, proj_bias, out_grad):
    width = block_in.shape[1]
    wqkv = qkv_weight.reshape(width, 3 * width)
    bias_row = jnp.concatenate([qv_bias[0], jnp.zeros_like(qv_bias[0]), qv_bias[1]])

    def one_sequence(carry, items):
        inputs, segs, upstream_gradient = items
        length = segs.shape[0]
        layer_input = inputs.astype(jnp.float32)
        first_norm_output, first_normalized_input, first_inverse_deviation = apply_layer_norm(layer_input, first_norm_gain, first_norm_bias)
        first_norm_output = first_norm_output.astype(jnp.bfloat16)
        qkv = (jnp.dot(first_norm_output, wqkv, preferred_element_type=jnp.float32) + bias_row).astype(jnp.bfloat16)
        parts = qkv.reshape(length, 3, HEADS, HD)
        query, key, value = (parts[:, 0], parts[:, 1], parts[:, 2])
        output, lse = attend(query, key, value, segs)
        flat = output.reshape(length, width)
        middle_state = layer_input + jnp.dot(flat, out_weight, preferred_element_type=jnp.float32) + out_bias
        second_norm_output, second_normalized_input, second_inverse_deviation = apply_layer_norm(middle_state, second_norm_gain, second_norm_bias)
        second_norm_output = second_norm_output.astype(jnp.bfloat16)
        pre = jnp.dot(second_norm_output, fc_weight, preferred_element_type=jnp.float32) + fc_bias
        act = gelu(pre).astype(jnp.bfloat16)
        result = middle_state + jnp.dot(act, proj_weight, preferred_element_type=jnp.float32) + proj_bias
        g_proj_w = jnp.dot(act.T, upstream_gradient, preferred_element_type=jnp.float32)
        cotf = upstream_gradient.astype(jnp.float32)
        g_proj_b = lax.optimization_barrier(jnp.sum(cotf, axis=0))
        d_pre = (jnp.dot(upstream_gradient, proj_weight.T, preferred_element_type=jnp.float32) * gelu_grad(pre)).astype(jnp.bfloat16)
        g_fc_w = jnp.dot(second_norm_output.T, d_pre, preferred_element_type=jnp.float32)
        g_fc_b = lax.optimization_barrier(jnp.sum(d_pre.astype(jnp.float32), axis=0))
        second_norm_gradient = jnp.dot(d_pre, fc_weight.T, preferred_element_type=jnp.float32)
        partial_gradient, second_norm_gain_gradient, second_norm_bias_gradient = layer_norm_backward(second_norm_gradient, second_normalized_input, second_inverse_deviation, second_norm_gain)
        d_mid = cotf + partial_gradient
        g_out_b = lax.optimization_barrier(jnp.sum(d_mid, axis=0))
        dmid_b = d_mid.astype(jnp.bfloat16)
        g_out_w = jnp.dot(flat.T, dmid_b, preferred_element_type=jnp.float32)
        d_o = jnp.dot(dmid_b, out_weight.T, preferred_element_type=jnp.float32).astype(jnp.bfloat16).reshape(length, HEADS, HD)
        d_query, d_key, d_value = attend_back(query, key, value, segs, output, lse, d_o)
        d_qkv = jnp.stack([d_query, d_key, d_value], axis=1).reshape(length, 3 * width)
        g_qkv_w = jnp.dot(first_norm_output.T, d_qkv, preferred_element_type=jnp.float32)
        g_qv_b = jnp.stack([lax.optimization_barrier(jnp.sum(d_query.astype(jnp.float32), axis=0)).reshape(width), lax.optimization_barrier(jnp.sum(d_value.astype(jnp.float32), axis=0)).reshape(width)])
        first_norm_gradient = jnp.dot(d_qkv, wqkv.T, preferred_element_type=jnp.float32)
        partial_gradient1, first_norm_gain_gradient, first_norm_bias_gradient = layer_norm_backward(first_norm_gradient, first_normalized_input, first_inverse_deviation, first_norm_gain)
        d_input = d_mid + partial_gradient1
        terms = (first_norm_gain_gradient, first_norm_bias_gradient, g_qkv_w, g_qv_b, g_out_w, g_out_b, second_norm_gain_gradient, second_norm_bias_gradient, g_fc_w, g_fc_b, g_proj_w, g_proj_b)
        carry = tuple((total + term for total, term in zip(carry, terms)))
        return (carry, (result, d_input))
    start = (jnp.zeros((width,), jnp.float32), jnp.zeros((width,), jnp.float32), jnp.zeros((width, 3 * width), jnp.float32), jnp.zeros((2, width), jnp.float32), jnp.zeros((width, width), jnp.float32), jnp.zeros((width,), jnp.float32), jnp.zeros((width,), jnp.float32), jnp.zeros((width,), jnp.float32), jnp.zeros((width, FF), jnp.float32), jnp.zeros((FF,), jnp.float32), jnp.zeros((FF, width), jnp.float32), jnp.zeros((width,), jnp.float32))
    count = segment_ids.shape[0]
    length = segment_ids.shape[1]
    items = (block_in.reshape(count, length, width), segment_ids, out_grad.reshape(count, length, width))
    sums, outputs = lax.scan(one_sequence, start, items)
    factor = 1.0 / count
    sums = tuple((total * factor for total in sums))
    result = outputs[0].reshape(count * length, width)
    d_input = outputs[1].reshape(count * length, width)
    return (result, d_input, sums[0], sums[1], sums[2].reshape(width, 3, width), sums[3], sums[4], sums[5], sums[6], sums[7], sums[8], sums[9], sums[10], sums[11])
```

```python
import math

import jax
import jax.numpy as jnp
from jax import lax
from jax.experimental import pallas as pl
from jax.experimental.pallas import tpu as pltpu
from jax.sharding import PartitionSpec as P

HD = 64


EPS = 1e-05
GELU_C = math.sqrt(2.0 / math.pi)


def apply_layer_norm(values, scale_gain, shift_bias):
    centered_input = values - jnp.mean(values, axis=-1, keepdims=True)
    variance = jnp.mean(centered_input * centered_input, axis=-1, keepdims=True)
    inverse_deviation = lax.rsqrt(variance + EPS)
    normalized_input = centered_input * inverse_deviation
    return (normalized_input * scale_gain + shift_bias, normalized_input, inverse_deviation)


def layer_norm_backward(upstream_gradient, normalized_input, inverse_deviation, scale_gain):
    scaled_gradient = upstream_gradient * scale_gain
    incoming_gradient = inverse_deviation * (
        scaled_gradient
        - jnp.mean(scaled_gradient, axis=-1, keepdims=True)
        - normalized_input * jnp.mean(scaled_gradient * normalized_input, axis=-1, keepdims=True)
    )
    return (
        incoming_gradient,
        jnp.sum(upstream_gradient * normalized_input, axis=0),
        jnp.sum(upstream_gradient, axis=0),
    )


def gelu(value):
    return 0.5 * value * (1.0 + jnp.tanh(GELU_C * (value + 0.044715 * value**3)))


def gelu_grad(value):
    tangent = jnp.tanh(GELU_C * (value + 0.044715 * value**3))
    return 0.5 * (1.0 + tangent) + 0.5 * value * (1.0 - tangent * tangent) * GELU_C * (
        1.0 + 3.0 * 0.044715 * value * value
    )


def gather_rows(values):
    return lax.all_gather(values, "tensor", axis=0, tiled=True)


def scatter_rows(values):
    return lax.psum_scatter(values, "tensor", scatter_dimension=0, tiled=True)


def masked_scores(query, key, segs):
    length = segs.shape[0]
    scores = jnp.einsum("qhd,khd->hqk", query, key, preferred_element_type=jnp.float32) * 0.125
    rows = jnp.arange(length)
    allowed = (segs[:, None] == segs[None, :]) & (rows[:, None] >= rows[None, :])
    return jnp.where(allowed[None], scores, -1e30)


def attend(items):
    query, key, value, segs = items
    scores = masked_scores(query, key, segs)
    top = jnp.max(scores, axis=-1, keepdims=True)
    lse = top[..., 0] + jnp.log(jnp.sum(jnp.exp(scores - top), axis=-1))
    weights = jnp.exp(scores - lse[..., None]).astype(jnp.bfloat16)
    output = jnp.einsum("hqk,khd->qhd", weights, value, preferred_element_type=jnp.float32)
    return (output.astype(jnp.bfloat16), lse)


def attend_back(items):
    query, key, value, segs, output, lse, d_out = items
    weights = jnp.exp(masked_scores(query, key, segs) - lse[..., None])
    rounded = weights.astype(jnp.bfloat16)
    d_value = jnp.einsum("hqk,qhd->khd", rounded, d_out, preferred_element_type=jnp.float32)
    d_probs = jnp.einsum("qhd,khd->hqk", d_out, value, preferred_element_type=jnp.float32)
    delta = jnp.transpose(jnp.sum(d_out.astype(jnp.float32) * output.astype(jnp.float32), axis=-1))
    d_scores = (weights * (d_probs - delta[..., None]) * 0.125).astype(jnp.bfloat16)
    d_query = jnp.einsum("hqk,khd->qhd", d_scores, key, preferred_element_type=jnp.float32)
    d_key = jnp.einsum("hqk,qhd->khd", d_scores, query, preferred_element_type=jnp.float32)
    return (d_query.astype(jnp.bfloat16), d_key.astype(jnp.bfloat16), d_value.astype(jnp.bfloat16))


def on_device(
    block_in,
    segment_ids,
    first_norm_gain,
    first_norm_bias,
    qkv_weight,
    qv_bias,
    out_weight,
    out_bias,
    second_norm_gain,
    second_norm_bias,
    fc_weight,
    fc_bias,
    proj_weight,
    proj_bias,
    out_grad,
):
    width = block_in.shape[1]
    local_width = qkv_weight.shape[2]
    heads_dev = local_width // HD
    seq_count = segment_ids.shape[0]
    length = segment_ids.shape[1]
    factor = 1.0 / (seq_count * lax.axis_size("dp"))
    wqkv = qkv_weight.reshape(width, 3 * local_width)
    bias_row = jnp.concatenate([qv_bias[0], jnp.zeros_like(qv_bias[0]), qv_bias[1]])
    layer_input = block_in.astype(jnp.float32)
    first_norm_output, first_normalized_input, first_inverse_deviation = apply_layer_norm(
        layer_input, first_norm_gain, first_norm_bias
    )
    full1 = gather_rows(first_norm_output.astype(jnp.bfloat16))
    qkv = (jnp.dot(full1, wqkv, preferred_element_type=jnp.float32) + bias_row).astype(jnp.bfloat16)
    parts = qkv.reshape(seq_count, length, 3, heads_dev, HD)
    query, key, value = (parts[:, :, 0], parts[:, :, 1], parts[:, :, 2])
    output, lse = lax.map(attend, (query, key, value, segment_ids))
    flat = output.reshape(seq_count * length, local_width)
    middle_state = (
        layer_input
        + scatter_rows(jnp.dot(flat, out_weight, preferred_element_type=jnp.float32))
        + out_bias
    )
    second_norm_output, second_normalized_input, second_inverse_deviation = apply_layer_norm(
        middle_state, second_norm_gain, second_norm_bias
    )
    full2 = gather_rows(second_norm_output.astype(jnp.bfloat16))
    pre = jnp.dot(full2, fc_weight, preferred_element_type=jnp.float32) + fc_bias
    act = gelu(pre).astype(jnp.bfloat16)
    block_out = (
        middle_state
        + scatter_rows(jnp.dot(act, proj_weight, preferred_element_type=jnp.float32))
        + proj_bias
    )
    grad_full = gather_rows(out_grad)
    g_proj_w = jnp.dot(act.T, grad_full, preferred_element_type=jnp.float32) * factor
    d_pre = (
        jnp.dot(grad_full, proj_weight.T, preferred_element_type=jnp.float32) * gelu_grad(pre)
    ).astype(jnp.bfloat16)
    g_fc_w = jnp.dot(full2.T, d_pre, preferred_element_type=jnp.float32) * factor
    g_fc_b = jnp.sum(d_pre.astype(jnp.float32), axis=0) * factor
    second_norm_gradient = scatter_rows(
        jnp.dot(d_pre, fc_weight.T, preferred_element_type=jnp.float32)
    )
    cotf = out_grad.astype(jnp.float32)
    partial_gradient, second_norm_gain_gradient, second_norm_bias_gradient = layer_norm_backward(
        second_norm_gradient, second_normalized_input, second_inverse_deviation, second_norm_gain
    )
    d_mid = cotf + partial_gradient
    g_proj_b = jnp.sum(cotf, axis=0) * factor
    g_out_b = jnp.sum(d_mid, axis=0) * factor
    mid_full = gather_rows(d_mid.astype(jnp.bfloat16))
    g_out_w = jnp.dot(flat.T, mid_full, preferred_element_type=jnp.float32) * factor
    d_o = jnp.dot(mid_full, out_weight.T, preferred_element_type=jnp.float32).astype(jnp.bfloat16)
    d_o = d_o.reshape(seq_count, length, heads_dev, HD)
    d_query, d_key, d_value = lax.map(
        attend_back, (query, key, value, segment_ids, output, lse, d_o)
    )
    d_qkv = jnp.stack([d_query, d_key, d_value], axis=2).reshape(
        seq_count * length, 3 * local_width
    )
    g_qkv_w = (jnp.dot(full1.T, d_qkv, preferred_element_type=jnp.float32) * factor).reshape(
        width, 3, local_width
    )
    query_sum = jnp.sum(d_query.astype(jnp.float32), axis=(0, 1)).reshape(local_width)
    value_sum = jnp.sum(d_value.astype(jnp.float32), axis=(0, 1)).reshape(local_width)
    g_qv_b = jnp.stack([query_sum, value_sum]) * factor
    first_norm_gradient = scatter_rows(jnp.dot(d_qkv, wqkv.T, preferred_element_type=jnp.float32))
    partial_gradient1, first_norm_gain_gradient, first_norm_bias_gradient = layer_norm_backward(
        first_norm_gradient, first_normalized_input, first_inverse_deviation, first_norm_gain
    )
    d_in = d_mid + partial_gradient1
    first_norm_gain_gradient = first_norm_gain_gradient * factor
    first_norm_bias_gradient = first_norm_bias_gradient * factor
    second_norm_gain_gradient = second_norm_gain_gradient * factor
    second_norm_bias_gradient = second_norm_bias_gradient * factor
    g_qkv_w, g_qv_b, g_out_w, g_proj_w, g_fc_w, g_fc_b = lax.psum(
        (g_qkv_w, g_qv_b, g_out_w, g_proj_w, g_fc_w, g_fc_b), "dp"
    )
    (
        first_norm_gain_gradient,
        first_norm_bias_gradient,
        g_out_b,
        second_norm_gain_gradient,
        second_norm_bias_gradient,
        g_proj_b,
    ) = lax.psum(
        (
            first_norm_gain_gradient,
            first_norm_bias_gradient,
            g_out_b,
            second_norm_gain_gradient,
            second_norm_bias_gradient,
            g_proj_b,
        ),
        ("dp", "tensor"),
    )
    return (
        block_out,
        d_in,
        first_norm_gain_gradient,
        first_norm_bias_gradient,
        g_qkv_w,
        g_qv_b,
        g_out_w,
        g_out_b,
        second_norm_gain_gradient,
        second_norm_bias_gradient,
        g_fc_w,
        g_fc_b,
        g_proj_w,
        g_proj_b,
    )


NT = 4
NC = 4
ROWS = 128
ORDER = (0, 3, 1, 2)
MESH = pl.DeviceIdType.MESH
F32 = jnp.float32
BF16 = jnp.bfloat16


def mm(a, b):
    return lax.dot_general(a, b, (((1,), (0,)), ((), ())), preferred_element_type=F32)


def mm_nt(a, b):
    return lax.dot_general(a, b, (((1,), (1,)), ((), ())), preferred_element_type=F32)


def mm_tn(a, b):
    return lax.dot_general(a, b, (((0,), (0,)), ((), ())), preferred_element_type=F32)


def norm_stats(values):
    centered = values - jnp.mean(values, axis=-1, keepdims=True)
    rstd = lax.rsqrt(jnp.mean(centered * centered, axis=-1, keepdims=True) + EPS)
    return centered * rstd, rstd


def norm_back(cot, xhat, rstd, gain):
    e = cot * gain
    return rstd * (
        e
        - jnp.mean(e, axis=-1, keepdims=True)
        - xhat * jnp.mean(e * xhat, axis=-1, keepdims=True)
    )


def layer_kernel(
    x_ref, g_ref, seg_col, seg_row, ln1, wqkv, bqkv, wout, ln2, wfc, bfc, wproj, bproj,
    bo_out, din_out, grad_out, vec_out,
    xfull, gfull, wfull, n1, qh, kh, vh, pscr, ofull, mid, n2, act, dpre,
    bo_send, dn2_send, dn1_send, bo_recv, dn2_recv, dn1_recv, dmid, dmid_own,
    dkacc, dvacc, dqkv, gl, d2d, hsum, rs, vsend, vbuf, wsend, wbuf,
    x_s, x_r, g_s, g_r, w1_s, w1_r, w2_s, w2_r, loc_s, o_s, o_r, n2_s, n2_r, n1_s, n1_r,
    b_s, b_r, m_s, m_r, d1_s, d1_r, rs_s, rs_r, ag_s, ag_r, d2_s, d2_r, va_s, va_r, vb_s, vb_r,
):
    d = lax.axis_index("dp")
    t = lax.axis_index("tensor")
    chip = d // 2
    core = d % 2

    def at_t(o):
        return (d, lax.rem(t + o, NT))

    def at_d(o):
        return (lax.rem(d + o, 8), t)

    def at_chip(o):
        return (lax.rem(chip + o, NC) * 2 + core, t)

    sibling = (chip * 2 + 1 - core, t)

    barrier = pltpu.get_barrier_semaphore()
    for o in range(1, NT):
        pl.semaphore_signal(barrier, inc=1, device_id=at_t(o), device_id_type=MESH)
    for o in range(1, 8):
        pl.semaphore_signal(barrier, inc=1, device_id=at_d(o), device_id_type=MESH)
    pl.semaphore_wait(barrier, NT - 1 + 7)

    pending = []

    def rcopy(src, dst, ss, rsem, dev):
        return pltpu.make_async_remote_copy(
            src_ref=src, dst_ref=dst, send_sem=ss, recv_sem=rsem, device_id=dev, device_id_type=MESH
        )

    def go(*args):
        c = rcopy(*args)
        c.start()
        pending.append(c)
        return c

    def rows_of(j):
        return pl.ds(pl.multiple_of(j * ROWS, ROWS), ROWS)

    cx = [go(x_ref, xfull.at[t], x_s.at[o], x_r.at[o], at_t(o)) for o in range(1, NT)]
    cols = pl.ds(pl.multiple_of(core * 384, 128), 384)
    wsrc = wout.at[pl.ds(pl.multiple_of(chip * 48, 16), 48), cols]
    own_w = pltpu.make_async_copy(wsrc, wfull.at[t, chip, :, cols], loc_s)
    own_w.start()
    cw1 = [
        go(wsrc, wfull.at[t, chip, :, cols], w1_s.at[o], w1_r.at[o], at_t(o))
        for o in range(1, NT)
    ]
    cg = [go(g_ref, gfull.at[t], g_s.at[o], g_r.at[o], at_t(o)) for o in range(1, NT)]
    xfull[t] = x_ref[...]
    gfull[t] = g_ref[...]

    for o in range(NT):
        if o:
            cx[o - 1].wait_recv()
        s = lax.rem(t + NT - o, NT)
        xhat, _ = norm_stats(xfull[s].astype(F32))
        nb = (xhat * ln1[0:1, :] + ln1[1:2, :]).astype(BF16)
        n1[rows_of(s), :] = nb
        qkv = (mm(nb, wqkv[...]) + bqkv[...]).astype(BF16)
        for h in range(3):
            qh[h, rows_of(s), :] = qkv[:, h * HD : h * HD + HD]
            kh[h, rows_of(s), :] = qkv[:, 192 + h * HD : 192 + h * HD + HD]
            vh[h, rows_of(s), :] = qkv[:, 384 + h * HD : 384 + h * HD + HD]

    own_w.wait()
    for c in cw1:
        c.wait_recv()
    wpart = wfull.at[:, chip, :, cols]
    cw2 = [go(wpart, wpart, w2_s.at[o], w2_r.at[o], at_d(o)) for o in range(1, 8)]

    co = {}
    for j in ORDER:
        r = slice(j * ROWS, (j + 1) * ROWS)
        n = (j + 1) * ROWS
        qi = j * ROWS + lax.broadcasted_iota(jnp.int32, (ROWS, n), 0)
        ki = lax.broadcasted_iota(jnp.int32, (ROWS, n), 1)
        allowed = (seg_col[r, :] == seg_row[:, :n]) & (qi >= ki)
        outs = []
        for h in range(3):
            sc = jnp.where(allowed, mm_nt(qh[h, r, :], kh[h, :n, :]) * 0.125, -1e30)
            e = jnp.exp(sc - jnp.max(sc, axis=-1, keepdims=True))
            p = e * (1.0 / jnp.sum(e, axis=-1, keepdims=True))
            pscr[h, r, :n] = p
            outs.append(mm(p.astype(BF16), vh[h, :n, :]))
        ofull[t, r, :] = jnp.concatenate(outs, axis=1).astype(BF16)
        co[j] = [
            go(ofull.at[t, r], ofull.at[t, r], o_s.at[j, o], o_r.at[j, o], at_t(o))
            for o in range(1, NT)
        ]

    for c in cw2:
        c.wait_recv()
    for c in cg:
        c.wait_recv()

    def send_block(buf, recv, ss, rsem, j):
        o = lax.rem(j - t + NT, NT)
        return rcopy(buf.at[j], recv.at[o], ss.at[j], rsem.at[o], (d, j))

    for j in ORDER:
        r = slice(j * ROWS, (j + 1) * ROWS)
        for c in co[j]:
            c.wait_recv()
        m = xfull[j].astype(F32) + ln2[2:3, :]
        for s in range(NT):
            m = m + mm(ofull[s, r, :], wfull[s].reshape(192, 768))
        mid[r, :] = m
        xhat, _ = norm_stats(m)
        nb = (xhat * ln2[0:1, :] + ln2[1:2, :]).astype(BF16)
        n2[r, :] = nb
        pre = mm(nb, wfc[...]) + bfc[...]
        sq = pre * pre
        tangent = jnp.tanh(GELU_C * (pre + 0.044715 * (sq * pre)))
        slope = 0.5 * (1.0 + tangent) + 0.5 * pre * (1.0 - tangent * tangent) * GELU_C * (
            1.0 + 3.0 * 0.044715 * sq
        )
        ab = (0.5 * pre * (1.0 + tangent)).astype(BF16)
        act[r, :] = ab
        dp = (mm_nt(gfull[j], wproj[...]) * slope).astype(BF16)
        dpre[r, :] = dp
        dn2_send[j] = mm_nt(dp, wfc[...]).astype(BF16)

        @pl.when(t != j)
        def _():
            send_block(dn2_send, dn2_recv, n2_s, n2_r, j).start()

        bo_send[j] = mm(ab, wproj[...]).astype(BF16)

    def stage1(i):
        half = pl.ds(pl.multiple_of((1 - core) * 384, 128), 384)
        return go(gl.at[i, half], d2d.at[i], d1_s.at[i], d1_r.at[i], sibling)

    def stage2(i, c):
        c.wait_recv()
        half = pl.ds(pl.multiple_of(core * 384, 128), 384)
        hsum[i] = (gl[i, half, :].astype(F32) + d2d[i].astype(F32)).astype(BF16)
        out = []
        for o in range(1, NC):
            to = pl.ds(pl.multiple_of(lax.rem(chip + o, NC) * 96, 32), 96)
            out.append(go(hsum.at[i, to], rs.at[i, o], rs_s.at[i, o], rs_r.at[i, o], at_chip(o)))
        return out

    def stage3(i, cs):
        own = pl.ds(pl.multiple_of(chip * 96, 32), 96)
        total = hsum[i, own, :].astype(F32)
        for o in range(1, NC):
            cs[o - 1].wait_recv()
            total = total + rs[i, o].astype(F32)
        at = pl.ds(pl.multiple_of(core * 384 + chip * 96, 32), 96)
        grad_out[i, at, :] = total.astype(BF16)
        blk = grad_out.at[i, at]
        return [
            go(blk, blk, ag_s.at[i, o], ag_r.at[i, o], at_chip(o)) for o in range(1, NC)
        ]

    def stage4(i, cs):
        for c in cs:
            c.wait_recv()
        half = grad_out.at[i, pl.ds(pl.multiple_of(core * 384, 128), 384)]
        return go(half, half, d2_s.at[i], d2_r.at[i], sibling)

    gmat = gfull[...].reshape(NT * ROWS, 768)
    gl[0] = mm_tn(act[...], gmat).astype(BF16)
    c1a = stage1(0)
    gl[1] = mm_tn(n2[...], dpre[...]).astype(BF16)
    c1b = stage1(1)

    def gathered(send, recv, ss, rsem):
        total = send[t].astype(F32)
        for o in range(1, NT):
            rcopy(send.at[0], recv.at[o], ss.at[0], rsem.at[o], at_t(o)).wait_recv()
            total = total + recv[o].astype(F32)
        return total

    own_rows = rows_of(t)
    gown = g_ref[...].astype(F32)
    dn2 = gathered(dn2_send, dn2_recv, n2_s, n2_r)
    xhat, rstd = norm_stats(mid[own_rows, :])
    dm = gown + norm_back(dn2, xhat, rstd, ln2[0:1, :])
    dmid_own[...] = dm
    dmid[t] = dm.astype(BF16)
    for o in range(1, NT):
        go(dmid.at[t], dmid.at[t], m_s.at[o], m_r.at[o], at_t(o))
    vsend[2:3, :] = jnp.sum(dm, axis=0, keepdims=True)
    vsend[3:4, :] = jnp.sum(dn2 * xhat, axis=0, keepdims=True)
    vsend[4:5, :] = jnp.sum(dn2, axis=0, keepdims=True)
    vsend[5:6, :] = jnp.sum(gown, axis=0, keepdims=True)
    vsend[6:7, :] = jnp.sum(dpre[...].astype(F32), axis=0, keepdims=True)
    for j in ORDER:

        @pl.when(t != j)
        def _():
            send_block(bo_send, bo_recv, b_s, b_r, j).start()

    c2a = stage2(0, c1a)
    c2b = stage2(1, c1b)

    dkacc[...] = jnp.zeros_like(dkacc)
    dvacc[...] = jnp.zeros_like(dvacc)
    for j in (3, 2, 1, 0):
        r = slice(j * ROWS, (j + 1) * ROWS)
        n = (j + 1) * ROWS

        @pl.when(t != j)
        def _():
            o = lax.rem(t - j + NT, NT)
            rcopy(dmid.at[j], dmid.at[j], m_s.at[o], m_r.at[o], (d, j)).wait_recv()

        do = mm_nt(dmid[j], wout[...]).astype(BF16)
        ob = ofull[t, r, :].astype(F32) * do.astype(F32)
        dq = []
        for h in range(3):
            hs = slice(h * HD, h * HD + HD)
            doh = do[:, hs]
            p = pscr[h, r, :n]
            dvacc[h, :n, :] += mm_tn(p.astype(BF16), doh)
            delta = jnp.sum(ob[:, hs], axis=-1, keepdims=True)
            ds = (p * (mm_nt(doh, vh[h, :n, :]) - delta) * 0.125).astype(BF16)
            dq.append(mm(ds, kh[h, :n, :]))
            dkacc[h, :n, :] += mm_tn(ds, qh[h, r, :])
        parts = dq + [dkacc[h, r, :] for h in range(3)] + [dvacc[h, r, :] for h in range(3)]
        dqkv[r, :] = jnp.concatenate(parts, axis=1).astype(BF16)
        dn1_send[j] = mm_nt(dqkv[r, :], wqkv[...]).astype(BF16)

        @pl.when(t != j)
        def _():
            send_block(dn1_send, dn1_recv, n1_s, n1_r, j).start()

        if j == 1:
            c3a = stage3(0, c2a)
            c3b = stage3(1, c2b)

    gl[2, :, 0:576] = mm_tn(n1[...], dqkv[...]).astype(BF16)
    dmat = dmid[...].reshape(NT * ROWS, 768)
    gl[2, :, 576:768] = mm_tn(dmat, ofull[t]).astype(BF16)
    c1c = stage1(2)
    dsum = jnp.sum(dqkv[...].astype(F32), axis=0, keepdims=True)
    vsend[7:8, :] = jnp.concatenate([dsum, jnp.zeros((1, 192), F32)], axis=1)
    c4a = stage4(0, c3a)
    c4b = stage4(1, c3b)
    c2c = stage2(2, c1c)
    bo = gathered(bo_send, bo_recv, b_s, b_r)
    bo_out[...] = mid[own_rows, :] + bo + bproj[...]
    dn1 = gathered(dn1_send, dn1_recv, n1_s, n1_r)
    xhat, rstd = norm_stats(x_ref[...].astype(F32))
    din_out[...] = dmid_own[...] + norm_back(dn1, xhat, rstd, ln1[0:1, :])
    vsend[0:1, :] = jnp.sum(dn1 * xhat, axis=0, keepdims=True)
    vsend[1:2, :] = jnp.sum(dn1, axis=0, keepdims=True)
    cva = [go(vsend, vbuf.at[t], va_s.at[o], va_r.at[o], at_t(o)) for o in range(1, NT)]
    vbuf[t] = vsend[...]
    c3c = stage3(2, c2c)
    for c in cva:
        c.wait_recv()
    wsend[...] = ((vbuf[0] + vbuf[1]) + vbuf[2]) + vbuf[3]
    wsend[6:8, :] = vsend[6:8, :]
    cvb = [go(wsend, wbuf.at[d], vb_s.at[o], vb_r.at[o], at_d(o)) for o in range(1, 8)]
    wbuf[d] = wsend[...]
    c4c = stage4(2, c3c)
    for c in cvb:
        c.wait_recv()
    total = wbuf[0]
    for s in range(1, 8):
        total = total + wbuf[s]
    vec_out[...] = total * 0.125
    c4a.wait_recv()
    c4b.wait_recv()
    c4c.wait_recv()

    for c in pending:
        c.wait_send()
    for j in range(NT):

        @pl.when(t != j)
        def _():
            send_block(dn2_send, dn2_recv, n2_s, n2_r, j).wait_send()
            send_block(bo_send, bo_recv, b_s, b_r, j).wait_send()
            send_block(dn1_send, dn1_recv, n1_s, n1_r, j).wait_send()


def on_device_fused(
    block_in, segment_ids, first_norm_gain, first_norm_bias, qkv_weight, qv_bias, out_weight,
    out_bias, second_norm_gain, second_norm_bias, fc_weight, fc_bias, proj_weight, proj_bias,
    out_grad,
):
    wqkv = qkv_weight.reshape(768, 576)
    bqkv = jnp.concatenate([qv_bias[0], jnp.zeros_like(qv_bias[0]), qv_bias[1]])[None]
    ln1 = jnp.stack([first_norm_gain, first_norm_bias])
    ln2 = jnp.stack([second_norm_gain, second_norm_bias, out_bias])
    full = lambda dt: pltpu.VMEM((NT, ROWS, 768), dt)
    head = lambda dt: pltpu.VMEM((3, 512, HD), dt)
    tall = lambda n, dt: pltpu.VMEM((512, n), dt)
    dma = lambda *s: pltpu.SemaphoreType.DMA(s)
    scratch = [
        full(BF16), full(BF16), pltpu.VMEM((NT, NC, 48, 768), BF16), tall(768, BF16),
        head(BF16), head(BF16), head(BF16), pltpu.VMEM((3, 512, 512), F32),
        pltpu.VMEM((NT, 512, 192), BF16), tall(768, F32), tall(768, BF16), tall(768, BF16),
        tall(768, BF16),
        full(BF16), full(BF16), full(BF16), full(BF16), full(BF16), full(BF16), full(BF16),
        pltpu.VMEM((ROWS, 768), F32),
        head(F32), head(F32), tall(576, BF16),
        pltpu.VMEM((3, 768, 768), BF16), pltpu.VMEM((3, 384, 768), BF16),
        pltpu.VMEM((3, 384, 768), BF16), pltpu.VMEM((3, NC, 96, 768), BF16),
        pltpu.VMEM((8, 768), F32), pltpu.VMEM((NT, 8, 768), F32),
        pltpu.VMEM((8, 768), F32), pltpu.VMEM((8, 8, 768), F32),
        dma(4), dma(4), dma(4), dma(4), dma(4), dma(4), dma(8), dma(8), pltpu.SemaphoreType.DMA,
        dma(4, 4), dma(4, 4), dma(4), dma(4), dma(4), dma(4), dma(4), dma(4), dma(4), dma(4),
        dma(3), dma(3), dma(3, 4), dma(3, 4), dma(3, 4), dma(3, 4), dma(3), dma(3),
        dma(4), dma(4), dma(8), dma(8),
    ]
    vm = pl.BlockSpec(memory_space=pltpu.VMEM)
    block_out, d_in, grads, vecs = pl.pallas_call(
        layer_kernel,
        out_shape=(
            jax.ShapeDtypeStruct((ROWS, 768), F32),
            jax.ShapeDtypeStruct((ROWS, 768), F32),
            jax.ShapeDtypeStruct((3, 768, 768), BF16),
            jax.ShapeDtypeStruct((8, 768), F32),
        ),
        in_specs=[vm] * 13,
        out_specs=[vm] * 4,
        scratch_shapes=scratch,
        compiler_params=pltpu.CompilerParams(
            collective_id=0, has_side_effects=True, vmem_limit_bytes=60 * 1024 * 1024
        ),
        cost_estimate=pl.CostEstimate(
            flops=8_000_000_000, bytes_accessed=12_000_000, transcendentals=2_000_000
        ),
    )(
        block_in, out_grad, segment_ids.reshape(512, 1), segment_ids, ln1, wqkv, bqkv, out_weight,
        ln2, fc_weight, fc_bias[None], proj_weight, proj_bias[None],
    )
    scaled = lambda a: a.astype(F32) * 0.125
    return (
        block_out,
        d_in,
        vecs[0],
        vecs[1],
        scaled(grads[2, :, :576]).reshape(768, 3, 192),
        jnp.stack([vecs[7, :192], vecs[7, 384:576]]),
        scaled(grads[2, :, 576:]).T,
        vecs[2],
        vecs[3],
        vecs[4],
        scaled(grads[1]),
        vecs[6],
        scaled(grads[0]),
        vecs[5],
    )


def solution(mesh):
    fits = mesh.shape["dp"] == 8 and mesh.shape["tensor"] == 4
    return jax.shard_map(
        on_device_fused if fits else on_device,
        mesh=mesh,
        in_specs=(
            P(("dp", "tensor"), None),
            P("dp", None),
            P(),
            P(),
            P(None, None, "tensor"),
            P(None, "tensor"),
            P("tensor", None),
            P(),
            P(),
            P(),
            P(None, "tensor"),
            P("tensor"),
            P("tensor", None),
            P(),
            P(("dp", "tensor"), None),
        ),
        out_specs=(
            P(("dp", "tensor"), None),
            P(("dp", "tensor"), None),
            P(),
            P(),
            P(None, None, "tensor"),
            P(None, "tensor"),
            P("tensor", None),
            P(),
            P(),
            P(),
            P(None, "tensor"),
            P("tensor"),
            P("tensor", None),
            P(),
        ),
        check_vma=False,
    )
```

```python
import math

import jax
import jax.numpy as jnp
from jax import lax
from jax.experimental import pallas as pl
from jax.experimental.pallas import tpu as pltpu
from jax.sharding import PartitionSpec as P

HD = 64


EPS = 1e-05
GELU_C = math.sqrt(2.0 / math.pi)


def apply_layer_norm(values, scale_gain, shift_bias):
    centered_input = values - jnp.mean(values, axis=-1, keepdims=True)
    variance = jnp.mean(centered_input * centered_input, axis=-1, keepdims=True)
    inverse_deviation = lax.rsqrt(variance + EPS)
    normalized_input = centered_input * inverse_deviation
    return (normalized_input * scale_gain + shift_bias, normalized_input, inverse_deviation)


def layer_norm_backward(upstream_gradient, normalized_input, inverse_deviation, scale_gain):
    scaled_gradient = upstream_gradient * scale_gain
    incoming_gradient = inverse_deviation * (
        scaled_gradient
        - jnp.mean(scaled_gradient, axis=-1, keepdims=True)
        - normalized_input * jnp.mean(scaled_gradient * normalized_input, axis=-1, keepdims=True)
    )
    return (
        incoming_gradient,
        jnp.sum(upstream_gradient * normalized_input, axis=0),
        jnp.sum(upstream_gradient, axis=0),
    )


def gelu(value):
    return 0.5 * value * (1.0 + jnp.tanh(GELU_C * (value + 0.044715 * value**3)))


def gelu_grad(value):
    tangent = jnp.tanh(GELU_C * (value + 0.044715 * value**3))
    return 0.5 * (1.0 + tangent) + 0.5 * value * (1.0 - tangent * tangent) * GELU_C * (
        1.0 + 3.0 * 0.044715 * value * value
    )


def gather_rows(values):
    return lax.all_gather(values, "tensor", axis=0, tiled=True)


def scatter_rows(values):
    return lax.psum_scatter(values, "tensor", scatter_dimension=0, tiled=True)


def masked_scores(query, key, segs):
    length = segs.shape[0]
    scores = jnp.einsum("qhd,khd->hqk", query, key, preferred_element_type=jnp.float32) * 0.125
    rows = jnp.arange(length)
    allowed = (segs[:, None] == segs[None, :]) & (rows[:, None] >= rows[None, :])
    return jnp.where(allowed[None], scores, -1e30)


def attend(items):
    query, key, value, segs = items
    scores = masked_scores(query, key, segs)
    top = jnp.max(scores, axis=-1, keepdims=True)
    lse = top[..., 0] + jnp.log(jnp.sum(jnp.exp(scores - top), axis=-1))
    weights = jnp.exp(scores - lse[..., None]).astype(jnp.bfloat16)
    output = jnp.einsum("hqk,khd->qhd", weights, value, preferred_element_type=jnp.float32)
    return (output.astype(jnp.bfloat16), lse)


def attend_back(items):
    query, key, value, segs, output, lse, d_out = items
    weights = jnp.exp(masked_scores(query, key, segs) - lse[..., None])
    rounded = weights.astype(jnp.bfloat16)
    d_value = jnp.einsum("hqk,qhd->khd", rounded, d_out, preferred_element_type=jnp.float32)
    d_probs = jnp.einsum("qhd,khd->hqk", d_out, value, preferred_element_type=jnp.float32)
    delta = jnp.transpose(jnp.sum(d_out.astype(jnp.float32) * output.astype(jnp.float32), axis=-1))
    d_scores = (weights * (d_probs - delta[..., None]) * 0.125).astype(jnp.bfloat16)
    d_query = jnp.einsum("hqk,khd->qhd", d_scores, key, preferred_element_type=jnp.float32)
    d_key = jnp.einsum("hqk,qhd->khd", d_scores, query, preferred_element_type=jnp.float32)
    return (d_query.astype(jnp.bfloat16), d_key.astype(jnp.bfloat16), d_value.astype(jnp.bfloat16))


def on_device(
    block_in,
    segment_ids,
    first_norm_gain,
    first_norm_bias,
    qkv_weight,
    qv_bias,
    out_weight,
    out_bias,
    second_norm_gain,
    second_norm_bias,
    fc_weight,
    fc_bias,
    proj_weight,
    proj_bias,
    out_grad,
):
    width = block_in.shape[1]
    local_width = qkv_weight.shape[2]
    heads_dev = local_width // HD
    seq_count = segment_ids.shape[0]
    length = segment_ids.shape[1]
    factor = 1.0 / (seq_count * lax.axis_size("dp"))
    wqkv = qkv_weight.reshape(width, 3 * local_width)
    bias_row = jnp.concatenate([qv_bias[0], jnp.zeros_like(qv_bias[0]), qv_bias[1]])
    layer_input = block_in.astype(jnp.float32)
    first_norm_output, first_normalized_input, first_inverse_deviation = apply_layer_norm(
        layer_input, first_norm_gain, first_norm_bias
    )
    full1 = gather_rows(first_norm_output.astype(jnp.bfloat16))
    qkv = (jnp.dot(full1, wqkv, preferred_element_type=jnp.float32) + bias_row).astype(jnp.bfloat16)
    parts = qkv.reshape(seq_count, length, 3, heads_dev, HD)
    query, key, value = (parts[:, :, 0], parts[:, :, 1], parts[:, :, 2])
    output, lse = lax.map(attend, (query, key, value, segment_ids))
    flat = output.reshape(seq_count * length, local_width)
    middle_state = (
        layer_input
        + scatter_rows(jnp.dot(flat, out_weight, preferred_element_type=jnp.float32))
        + out_bias
    )
    second_norm_output, second_normalized_input, second_inverse_deviation = apply_layer_norm(
        middle_state, second_norm_gain, second_norm_bias
    )
    full2 = gather_rows(second_norm_output.astype(jnp.bfloat16))
    pre = jnp.dot(full2, fc_weight, preferred_element_type=jnp.float32) + fc_bias
    act = gelu(pre).astype(jnp.bfloat16)
    block_out = (
        middle_state
        + scatter_rows(jnp.dot(act, proj_weight, preferred_element_type=jnp.float32))
        + proj_bias
    )
    grad_full = gather_rows(out_grad)
    g_proj_w = jnp.dot(act.T, grad_full, preferred_element_type=jnp.float32) * factor
    d_pre = (
        jnp.dot(grad_full, proj_weight.T, preferred_element_type=jnp.float32) * gelu_grad(pre)
    ).astype(jnp.bfloat16)
    g_fc_w = jnp.dot(full2.T, d_pre, preferred_element_type=jnp.float32) * factor
    g_fc_b = jnp.sum(d_pre.astype(jnp.float32), axis=0) * factor
    second_norm_gradient = scatter_rows(
        jnp.dot(d_pre, fc_weight.T, preferred_element_type=jnp.float32)
    )
    cotf = out_grad.astype(jnp.float32)
    partial_gradient, second_norm_gain_gradient, second_norm_bias_gradient = layer_norm_backward(
        second_norm_gradient, second_normalized_input, second_inverse_deviation, second_norm_gain
    )
    d_mid = cotf + partial_gradient
    g_proj_b = jnp.sum(cotf, axis=0) * factor
    g_out_b = jnp.sum(d_mid, axis=0) * factor
    mid_full = gather_rows(d_mid.astype(jnp.bfloat16))
    g_out_w = jnp.dot(flat.T, mid_full, preferred_element_type=jnp.float32) * factor
    d_o = jnp.dot(mid_full, out_weight.T, preferred_element_type=jnp.float32).astype(jnp.bfloat16)
    d_o = d_o.reshape(seq_count, length, heads_dev, HD)
    d_query, d_key, d_value = lax.map(
        attend_back, (query, key, value, segment_ids, output, lse, d_o)
    )
    d_qkv = jnp.stack([d_query, d_key, d_value], axis=2).reshape(
        seq_count * length, 3 * local_width
    )
    g_qkv_w = (jnp.dot(full1.T, d_qkv, preferred_element_type=jnp.float32) * factor).reshape(
        width, 3, local_width
    )
    query_sum = jnp.sum(d_query.astype(jnp.float32), axis=(0, 1)).reshape(local_width)
    value_sum = jnp.sum(d_value.astype(jnp.float32), axis=(0, 1)).reshape(local_width)
    g_qv_b = jnp.stack([query_sum, value_sum]) * factor
    first_norm_gradient = scatter_rows(jnp.dot(d_qkv, wqkv.T, preferred_element_type=jnp.float32))
    partial_gradient1, first_norm_gain_gradient, first_norm_bias_gradient = layer_norm_backward(
        first_norm_gradient, first_normalized_input, first_inverse_deviation, first_norm_gain
    )
    d_in = d_mid + partial_gradient1
    first_norm_gain_gradient = first_norm_gain_gradient * factor
    first_norm_bias_gradient = first_norm_bias_gradient * factor
    second_norm_gain_gradient = second_norm_gain_gradient * factor
    second_norm_bias_gradient = second_norm_bias_gradient * factor
    g_qkv_w, g_qv_b, g_out_w, g_proj_w, g_fc_w, g_fc_b = lax.psum(
        (g_qkv_w, g_qv_b, g_out_w, g_proj_w, g_fc_w, g_fc_b), "dp"
    )
    (
        first_norm_gain_gradient,
        first_norm_bias_gradient,
        g_out_b,
        second_norm_gain_gradient,
        second_norm_bias_gradient,
        g_proj_b,
    ) = lax.psum(
        (
            first_norm_gain_gradient,
            first_norm_bias_gradient,
            g_out_b,
            second_norm_gain_gradient,
            second_norm_bias_gradient,
            g_proj_b,
        ),
        ("dp", "tensor"),
    )
    return (
        block_out,
        d_in,
        first_norm_gain_gradient,
        first_norm_bias_gradient,
        g_qkv_w,
        g_qv_b,
        g_out_w,
        g_out_b,
        second_norm_gain_gradient,
        second_norm_bias_gradient,
        g_fc_w,
        g_fc_b,
        g_proj_w,
        g_proj_b,
    )


NT = 4
NC = 4
ROWS = 128
ORDER = (0, 3, 1, 2)
BACK = (3, 2, 1, 0)
MESH = pl.DeviceIdType.MESH
F32 = jnp.float32
BF16 = jnp.bfloat16


def mm(a, b):
    return lax.dot_general(a, b, (((1,), (0,)), ((), ())), preferred_element_type=F32)


def mm_nt(a, b):
    return lax.dot_general(a, b, (((1,), (1,)), ((), ())), preferred_element_type=F32)


def mm_tn(a, b):
    return lax.dot_general(a, b, (((0,), (0,)), ((), ())), preferred_element_type=F32)


def norm_stats(values):
    centered = values - jnp.mean(values, axis=-1, keepdims=True)
    rstd = lax.rsqrt(jnp.mean(centered * centered, axis=-1, keepdims=True) + EPS)
    return centered * rstd, rstd


def norm_back(cot, xhat, rstd, gain):
    e = cot * gain
    return rstd * (
        e
        - jnp.mean(e, axis=-1, keepdims=True)
        - xhat * jnp.mean(e * xhat, axis=-1, keepdims=True)
    )


def layer_kernel(
    x_ref, g_ref, seg_row, gain1, shift1, wqkv, qvb, wout, bout, gain2, shift2, wfc, bfc, wproj, bproj,
    bo_out, din_out, grad_out, vec_out, qv_out,
    xfull, gfull, wfull, n1, qh, kh, vh, pscr, ofull, mid, n2, act, dpre,
    bo_send, dn2_send, dn1_send, bo_recv, dn2_recv, dn1_recv, dmid, dmid_own,
    dkacc, dvacc, dqkv, gl, d2d, hsum, rs, vsend, vbuf, wsend, wbuf,
    x_s, x_r, g_s, g_r, w1_s, w1_r, w2_s, w2_r, loc_s, o_s, o_r, n2_s, n2_r, n1_s, n1_r,
    b_s, b_r, m_s, m_r, d1_s, d1_r, rs_s, rs_r, ag_s, ag_r, d2_s, d2_r, va_s, va_r, vb_s, vb_r,
):
    d = lax.axis_index("dp")
    t = lax.axis_index("tensor")
    chip = d // 2
    core = d % 2

    def at_t(o):
        return (d, lax.rem(t + o, NT))

    def at_d(o):
        return (lax.rem(d + o, 8), t)

    def at_chip(o):
        return (lax.rem(chip + o, NC) * 2 + core, t)

    sibling = (chip * 2 + 1 - core, t)

    barrier = pltpu.get_barrier_semaphore()
    for o in range(1, NT):
        pl.semaphore_signal(barrier, inc=1, device_id=at_t(o), device_id_type=MESH)
    for o in range(1, 8):
        pl.semaphore_signal(barrier, inc=1, device_id=at_d(o), device_id_type=MESH)
    pl.semaphore_wait(barrier, NT - 1 + 7)

    pending = []
    ln1 = (gain1[...][None], shift1[...][None])
    ln2 = (gain2[...][None], shift2[...][None], bout[...][None])
    bqkv = jnp.concatenate([qvb[0:1, :], jnp.zeros((1, 192), F32), qvb[1:2, :]], axis=1)
    bfc_row = bfc[...][None]
    seg_col = jnp.transpose(jnp.broadcast_to(seg_row[...].astype(F32), (ROWS, 512)))[:, 0:1]
    seg_line = seg_row[...].astype(F32)

    def rcopy(src, dst, ss, rsem, dev):
        return pltpu.make_async_remote_copy(
            src_ref=src, dst_ref=dst, send_sem=ss, recv_sem=rsem, device_id=dev, device_id_type=MESH
        )

    def go(*args):
        c = rcopy(*args)
        c.start()
        pending.append(c)
        return c

    def rows_of(j):
        return pl.ds(pl.multiple_of(j * ROWS, ROWS), ROWS)

    def hop_send(k, ref, ss, rsem, r=None):
        def go_to(cond, slot, side, to):
            @pl.when(cond)
            def _():
                b = ref.at[slot] if r is None else ref.at[slot, r]
                rcopy(b, b, ss.at[side, k], rsem.at[side, k], (d, to)).start()

        go_to((t < NT - 1) & (t >= k), t - k, 0, t + 1)
        go_to((t > 0) & (t + k < NT), t + k, 1, t - 1)

    def hop_wait(k, ref, ss, rsem, r=None):
        b = ref.at[0] if r is None else ref.at[0, r]

        @pl.when(t >= k + 1)
        def _():
            rcopy(b, b, ss.at[0, k], rsem.at[0, k], at_t(1)).wait_recv()

        @pl.when(t + k + 1 < NT)
        def _():
            rcopy(b, b, ss.at[1, k], rsem.at[1, k], at_t(1)).wait_recv()

    def hop_sent(ref, ss, rsem, r=None):
        b = ref.at[0] if r is None else ref.at[0, r]
        for k in range(NT - 1):

            @pl.when((t < NT - 1) & (t >= k))
            def _():
                rcopy(b, b, ss.at[0, k], rsem.at[0, k], at_t(1)).wait_send()

            @pl.when((t > 0) & (t + k < NT))
            def _():
                rcopy(b, b, ss.at[1, k], rsem.at[1, k], at_t(1)).wait_send()

    def sum_hop(k, j, send, recv, ss, rsem):
        for side, here, to in ((0, k, 1), (1, NT - 1 - k, -1)):
            if (here < j) if side == 0 else (here > j):

                @pl.when(t == here)
                def _():
                    c = rcopy(
                        send.at[j], recv.at[side, j], ss.at[j], rsem.at[side, j], (d, here + to)
                    )
                    if k:
                        c.wait_recv()
                        send[j] = (send[j].astype(F32) + recv[side, j].astype(F32)).astype(BF16)
                    c.start()

    def sum_steps(i, order, *bufs):
        for k in range(NT - 1):
            if 0 <= i - k < NT:
                sum_hop(k, order[i - k], *bufs)

    def sum_ends(recv):
        @pl.when(t == 0)
        def _():
            recv[0, 0] = jnp.zeros((ROWS, 768), BF16)

        @pl.when(t == NT - 1)
        def _():
            recv[1, NT - 1] = jnp.zeros((ROWS, 768), BF16)

    def gathered(send, recv, ss, rsem):
        @pl.when(t > 0)
        def _():
            rcopy(send.at[t], recv.at[0, t], ss.at[t], rsem.at[0, t], at_t(1)).wait_recv()

        @pl.when(t < NT - 1)
        def _():
            rcopy(send.at[t], recv.at[1, t], ss.at[t], rsem.at[1, t], at_t(1)).wait_recv()

        return send[t].astype(F32) + recv[0, t].astype(F32) + recv[1, t].astype(F32)

    xfull[t] = x_ref[...]
    gfull[t] = g_ref[...]
    hop_send(0, xfull, x_s, x_r)
    cols = pl.ds(pl.multiple_of(core * 384, 128), 384)
    wsrc = wout.at[pl.ds(pl.multiple_of(chip * 48, 16), 48), cols]
    own_w = pltpu.make_async_copy(wsrc, wfull.at[t, chip, :, cols], loc_s)
    own_w.start()
    cw1 = [
        go(wsrc, wfull.at[t, chip, :, cols], w1_s.at[o], w1_r.at[o], at_t(o))
        for o in range(1, NT)
    ]
    for buf in (bo_recv, dn2_recv, dn1_recv):
        sum_ends(buf)

    def project(s):
        xhat, _ = norm_stats(xfull[s].astype(F32))
        nb = (xhat * ln1[0] + ln1[1]).astype(BF16)
        n1[rows_of(s), :] = nb
        qkv = (mm_nt(nb, wqkv[...]) + bqkv).astype(BF16)
        for h in range(3):
            qh[h, rows_of(s), :] = qkv[:, h * HD : h * HD + HD]
            kh[h, rows_of(s), :] = qkv[:, 192 + h * HD : 192 + h * HD + HD]
            vh[h, rows_of(s), :] = qkv[:, 384 + h * HD : 384 + h * HD + HD]

    project(t)
    hop_wait(0, xfull, x_s, x_r)
    hop_send(1, xfull, x_s, x_r)
    near = t + 1 - 2 * lax.rem(t, 2)
    project(near)
    hop_wait(1, xfull, x_s, x_r)
    hop_send(2, xfull, x_s, x_r)
    hop_send(0, gfull, g_s, g_r)
    own_w.wait()
    for c in cw1:
        c.wait_recv()
    wpart = wfull.at[:, chip, :, cols]
    hop_wait(2, xfull, x_s, x_r)
    far = lax.rem(t + 2, NT)
    project(far)
    project(far + 1 - 2 * lax.rem(far, 2))
    hop_wait(0, gfull, g_s, g_r)
    hop_send(1, gfull, g_s, g_r)
    cw2 = [go(wpart, wpart, w2_s.at[o], w2_r.at[o], at_d(o)) for o in range(1, 8)]

    def o_hops(i):
        for k in range(NT):
            if 0 <= i - k < NT:
                j = ORDER[i - k]
                args = (ofull, o_s.at[j], o_r.at[j], slice(j * ROWS, (j + 1) * ROWS))
                if k:
                    hop_wait(k - 1, *args)
                if k < NT - 1:
                    hop_send(k, *args)

    for i, j in enumerate(ORDER):
        r = slice(j * ROWS, (j + 1) * ROWS)
        n = (j + 1) * ROWS
        qi = j * ROWS + lax.broadcasted_iota(jnp.int32, (ROWS, n), 0)
        ki = lax.broadcasted_iota(jnp.int32, (ROWS, n), 1)
        allowed = (seg_col[r, :] == seg_line[:, :n]) & (qi >= ki)
        outs = []
        for h in range(3):
            sc = jnp.where(allowed, mm_nt(qh[h, r, :], kh[h, :n, :]) * 0.125, -1e30)
            e = jnp.exp(sc - jnp.max(sc, axis=-1, keepdims=True))
            p = e * (1.0 / jnp.sum(e, axis=-1, keepdims=True))
            pscr[h, r, :n] = p
            outs.append(mm(p.astype(BF16), vh[h, :n, :]))
        ofull[t, r, :] = jnp.concatenate(outs, axis=1).astype(BF16)
        o_hops(i)
        if i == 1:
            hop_wait(1, gfull, g_s, g_r)
            hop_send(2, gfull, g_s, g_r)

    for c in cw2:
        c.wait_recv()
    hop_wait(2, gfull, g_s, g_r)

    dn2_sum = (dn2_send, dn2_recv, n2_s, n2_r)
    bo_sum = (bo_send, bo_recv, b_s, b_r)
    dn1_sum = (dn1_send, dn1_recv, n1_s, n1_r)
    for i, j in enumerate(ORDER):
        r = slice(j * ROWS, (j + 1) * ROWS)
        if i:
            o_hops(i + 3)
        m = xfull[j].astype(F32) + ln2[2]
        for s in range(NT):
            m = m + mm(ofull[s, r, :], wfull[s].reshape(192, 768))
        mid[r, :] = m
        xhat, _ = norm_stats(m)
        nb = (xhat * ln2[0] + ln2[1]).astype(BF16)
        n2[r, :] = nb
        pre = mm(nb, wfc[...]) + bfc_row
        sq = pre * pre
        tangent = jnp.tanh(GELU_C * (pre + 0.044715 * (sq * pre)))
        slope = 0.5 * (1.0 + tangent) + 0.5 * pre * (1.0 - tangent * tangent) * GELU_C * (
            1.0 + 3.0 * 0.044715 * sq
        )
        ab = (0.5 * pre * (1.0 + tangent)).astype(BF16)
        act[r, :] = ab
        dp = (mm_nt(gfull[j], wproj[...]) * slope).astype(BF16)
        dpre[r, :] = dp
        dn2_send[j] = mm_nt(dp, wfc[...]).astype(BF16)

        sum_steps(i, ORDER, *dn2_sum)
        bo_send[j] = mm(ab, wproj[...]).astype(BF16)

    def stage1(i):
        half = pl.ds(pl.multiple_of((1 - core) * 384, 128), 384)
        return go(gl.at[i, half], d2d.at[i], d1_s.at[i], d1_r.at[i], sibling)

    def stage2(i, c):
        c.wait_recv()
        half = pl.ds(pl.multiple_of(core * 384, 128), 384)
        hsum[i] = (gl[i, half, :].astype(F32) + d2d[i].astype(F32)).astype(BF16)
        out = []
        for o in range(1, NC):
            to = pl.ds(pl.multiple_of(lax.rem(chip + o, NC) * 96, 32), 96)
            out.append(go(hsum.at[i, to], rs.at[i, o], rs_s.at[i, o], rs_r.at[i, o], at_chip(o)))
        return out

    def stage3(i, cs):
        own = pl.ds(pl.multiple_of(chip * 96, 32), 96)
        total = hsum[i, own, :].astype(F32)
        for o in range(1, NC):
            cs[o - 1].wait_recv()
            total = total + rs[i, o].astype(F32)
        at = pl.ds(pl.multiple_of(core * 384 + chip * 96, 32), 96)
        grad_out[i, at, :] = total.astype(BF16)
        blk = grad_out.at[i, at]
        return [
            go(blk, blk, ag_s.at[i, o], ag_r.at[i, o], at_chip(o)) for o in range(1, NC)
        ]

    def stage4(i, cs):
        for c in cs:
            c.wait_recv()
        half = grad_out.at[i, pl.ds(pl.multiple_of(core * 384, 128), 384)]
        return go(half, half, d2_s.at[i], d2_r.at[i], sibling)

    sum_steps(4, ORDER, *dn2_sum)
    gmat = gfull[...].reshape(NT * ROWS, 768)
    gl[0] = mm_tn(act[...], gmat).astype(BF16)
    c1a = stage1(0)
    sum_steps(5, ORDER, *dn2_sum)

    own_rows = rows_of(t)
    gown = g_ref[...].astype(F32)
    dn2 = gathered(*dn2_sum)
    xhat, rstd = norm_stats(mid[own_rows, :])
    dm = gown + norm_back(dn2, xhat, rstd, ln2[0])
    dmid_own[...] = dm
    dmid[t] = dm.astype(BF16)
    hop_send(0, dmid, m_s, m_r)
    sum_steps(0, ORDER, *bo_sum)
    sum_steps(1, ORDER, *bo_sum)
    vsend[2:3, :] = jnp.sum(dm, axis=0, keepdims=True)
    vsend[3:4, :] = jnp.sum(dn2 * xhat, axis=0, keepdims=True)
    vsend[4:5, :] = jnp.sum(dn2, axis=0, keepdims=True)
    vsend[5:6, :] = jnp.sum(gown, axis=0, keepdims=True)
    vsend[6:7, :] = jnp.sum(dpre[...].astype(F32), axis=0, keepdims=True)
    hop_wait(0, dmid, m_s, m_r)
    hop_send(1, dmid, m_s, m_r)
    gl[1] = mm_tn(n2[...], dpre[...]).astype(BF16)
    c1b = stage1(1)
    c2a = stage2(0, c1a)
    hop_wait(1, dmid, m_s, m_r)
    hop_send(2, dmid, m_s, m_r)
    c2b = stage2(1, c1b)
    sum_steps(2, ORDER, *bo_sum)
    sum_steps(3, ORDER, *bo_sum)
    hop_wait(2, dmid, m_s, m_r)

    dkacc[...] = jnp.zeros_like(dkacc)
    dvacc[...] = jnp.zeros_like(dvacc)
    for i, j in enumerate(BACK):
        r = slice(j * ROWS, (j + 1) * ROWS)
        n = (j + 1) * ROWS

        do = mm_nt(dmid[j], wout[...]).astype(BF16)
        ob = ofull[t, r, :].astype(F32) * do.astype(F32)
        dq = []
        for h in range(3):
            hs = slice(h * HD, h * HD + HD)
            doh = do[:, hs]
            p = pscr[h, r, :n]
            dvacc[h, :n, :] += mm_tn(p.astype(BF16), doh)
            delta = jnp.sum(ob[:, hs], axis=-1, keepdims=True)
            ds = (p * (mm_nt(doh, vh[h, :n, :]) - delta) * 0.125).astype(BF16)
            dq.append(mm(ds, kh[h, :n, :]))
            dkacc[h, :n, :] += mm_tn(ds, qh[h, r, :])
        parts = dq + [dkacc[h, r, :] for h in range(3)] + [dvacc[h, r, :] for h in range(3)]
        dqkv[r, :] = jnp.concatenate(parts, axis=1).astype(BF16)
        dn1_send[j] = mm(dqkv[r, :], wqkv[...]).astype(BF16)
        sum_steps(i, BACK, *dn1_sum)

        if j == 1:
            c3a = stage3(0, c2a)
            c3b = stage3(1, c2b)

    gl[2, 0:576, :] = mm_tn(dqkv[...], n1[...]).astype(BF16)
    gl[2, 576:768, :] = mm_tn(ofull[t], dmid[...].reshape(NT * ROWS, 768)).astype(BF16)
    c1c = stage1(2)
    sum_steps(4, BACK, *dn1_sum)
    dsum = jnp.sum(dqkv[...].astype(F32), axis=0, keepdims=True)
    vsend[7:8, :] = jnp.concatenate([dsum, jnp.zeros((1, 192), F32)], axis=1)
    c4a = stage4(0, c3a)
    c4b = stage4(1, c3b)
    c2c = stage2(2, c1c)
    sum_steps(5, BACK, *dn1_sum)
    sum_steps(4, ORDER, *bo_sum)
    sum_steps(5, ORDER, *bo_sum)
    bo = gathered(*bo_sum)
    bo_out[...] = mid[own_rows, :] + bo + bproj[...][None]
    dn1 = gathered(*dn1_sum)
    xhat, rstd = norm_stats(x_ref[...].astype(F32))
    din_out[...] = dmid_own[...] + norm_back(dn1, xhat, rstd, ln1[0])
    vsend[0:1, :] = jnp.sum(dn1 * xhat, axis=0, keepdims=True)
    vsend[1:2, :] = jnp.sum(dn1, axis=0, keepdims=True)
    cva = [go(vsend, vbuf.at[t], va_s.at[o], va_r.at[o], at_t(o)) for o in range(1, NT)]
    vbuf[t] = vsend[...]
    c3c = stage3(2, c2c)
    for c in cva:
        c.wait_recv()
    wsend[...] = ((vbuf[0] + vbuf[1]) + vbuf[2]) + vbuf[3]
    wsend[6:8, :] = vsend[6:8, :]
    cvb = [go(wsend, wbuf.at[d], vb_s.at[o], vb_r.at[o], at_d(o)) for o in range(1, 8)]
    wbuf[d] = wsend[...]
    c4c = stage4(2, c3c)
    for c in cvb:
        c.wait_recv()
    total = wbuf[0]
    for s in range(1, 8):
        total = total + wbuf[s]
    total = total * 0.125
    vec_out[...] = total
    qv_out[0:1, :] = total[7:8, 0:192]
    qv_out[1:2, :] = total[7:8, 384:576]
    c4a.wait_recv()
    c4b.wait_recv()
    c4c.wait_recv()

    for c in pending:
        c.wait_send()
    for args in ((xfull, x_s, x_r), (gfull, g_s, g_r), (dmid, m_s, m_r)):
        hop_sent(*args)
    for j in range(NT):
        hop_sent(ofull, o_s.at[j], o_r.at[j], slice(j * ROWS, (j + 1) * ROWS))

        @pl.when(t != j)
        def _():
            for send, recv, ss, rsem in (dn2_sum, bo_sum, dn1_sum):
                rcopy(send.at[j], recv.at[0, j], ss.at[j], rsem.at[0, j], at_t(1)).wait_send()


def on_device_fused(
    block_in, segment_ids, first_norm_gain, first_norm_bias, qkv_weight, qv_bias, out_weight,
    out_bias, second_norm_gain, second_norm_bias, fc_weight, fc_bias, proj_weight, proj_bias,
    out_grad,
):
    wqkv = jnp.transpose(qkv_weight, (1, 2, 0)).reshape(576, 768)
    full = lambda dt: pltpu.VMEM((NT, ROWS, 768), dt)
    head = lambda dt: pltpu.VMEM((3, 512, HD), dt)
    tall = lambda n, dt: pltpu.VMEM((512, n), dt)
    dma = lambda *s: pltpu.SemaphoreType.DMA(s)
    pair = pltpu.VMEM((2, NT, ROWS, 768), BF16)
    hops = (2, NT - 1)
    scratch = [
        full(BF16), full(BF16), pltpu.VMEM((NT, NC, 48, 768), BF16), tall(768, BF16),
        head(BF16), head(BF16), head(BF16), pltpu.VMEM((3, 512, 512), F32),
        pltpu.VMEM((NT, 512, 192), BF16), tall(768, F32), tall(768, BF16), tall(768, BF16),
        tall(768, BF16),
        full(BF16), full(BF16), full(BF16), pair, pair, pair, full(BF16),
        pltpu.VMEM((ROWS, 768), F32),
        head(F32), head(F32), tall(576, BF16),
        pltpu.VMEM((3, 768, 768), BF16), pltpu.VMEM((3, 384, 768), BF16),
        pltpu.VMEM((3, 384, 768), BF16), pltpu.VMEM((3, NC, 96, 768), BF16),
        pltpu.VMEM((8, 768), F32), pltpu.VMEM((NT, 8, 768), F32),
        pltpu.VMEM((8, 768), F32), pltpu.VMEM((8, 8, 768), F32),
        dma(*hops), dma(*hops), dma(*hops), dma(*hops), dma(4), dma(4), dma(8), dma(8), pltpu.SemaphoreType.DMA,
        dma(4, *hops), dma(4, *hops), dma(4), dma(2, 4), dma(4), dma(2, 4), dma(4), dma(2, 4),
        dma(*hops), dma(*hops),
        dma(3), dma(3), dma(3, 4), dma(3, 4), dma(3, 4), dma(3, 4), dma(3), dma(3),
        dma(4), dma(4), dma(8), dma(8),
    ]
    vm = pl.BlockSpec(memory_space=pltpu.VMEM)
    block_out, d_in, grads, vecs, qv = pl.pallas_call(
        layer_kernel,
        out_shape=(
            jax.ShapeDtypeStruct((ROWS, 768), F32),
            jax.ShapeDtypeStruct((ROWS, 768), F32),
            jax.ShapeDtypeStruct((3, 768, 768), BF16),
            jax.ShapeDtypeStruct((8, 768), F32),
            jax.ShapeDtypeStruct((2, 192), F32),
        ),
        in_specs=[vm] * 15,
        out_specs=[vm] * 5,
        scratch_shapes=scratch,
        compiler_params=pltpu.CompilerParams(
            collective_id=0, has_side_effects=True, vmem_limit_bytes=60 * 1024 * 1024
        ),
        cost_estimate=pl.CostEstimate(
            flops=8_000_000_000, bytes_accessed=12_000_000, transcendentals=2_000_000
        ),
    )(
        block_in, out_grad, segment_ids, first_norm_gain, first_norm_bias, wqkv, qv_bias,
        out_weight, out_bias, second_norm_gain, second_norm_bias, fc_weight, fc_bias, proj_weight,
        proj_bias,
    )
    scaled = lambda a: a.astype(F32) * 0.125
    return (
        block_out,
        d_in,
        vecs[0],
        vecs[1],
        jnp.transpose(scaled(grads[2, :576]).reshape(3, 192, 768), (2, 0, 1)),
        qv,
        scaled(grads[2, 576:]),
        vecs[2],
        vecs[3],
        vecs[4],
        scaled(grads[1]),
        vecs[6],
        scaled(grads[0]),
        vecs[5],
    )


def solution(mesh):
    fits = mesh.shape["dp"] == 8 and mesh.shape["tensor"] == 4
    return jax.shard_map(
        on_device_fused if fits else on_device,
        mesh=mesh,
        in_specs=(
            P(("dp", "tensor"), None),
            P("dp", None),
            P(),
            P(),
            P(None, None, "tensor"),
            P(None, "tensor"),
            P("tensor", None),
            P(),
            P(),
            P(),
            P(None, "tensor"),
            P("tensor"),
            P("tensor", None),
            P(),
            P(("dp", "tensor"), None),
        ),
        out_specs=(
            P(("dp", "tensor"), None),
            P(("dp", "tensor"), None),
            P(),
            P(),
            P(None, None, "tensor"),
            P(None, "tensor"),
            P("tensor", None),
            P(),
            P(),
            P(),
            P(None, "tensor"),
            P("tensor"),
            P("tensor", None),
            P(),
        ),
        check_vma=False,
    )
```

```python
import math

import jax
import jax.numpy as jnp
from jax import lax
from jax.experimental import pallas as pl
from jax.experimental.pallas import tpu as pltpu
from jax.sharding import PartitionSpec as P

HD = 64


EPS = 1e-05
GELU_C = math.sqrt(2.0 / math.pi)


def apply_layer_norm(values, scale_gain, shift_bias):
    centered_input = values - jnp.mean(values, axis=-1, keepdims=True)
    variance = jnp.mean(centered_input * centered_input, axis=-1, keepdims=True)
    inverse_deviation = lax.rsqrt(variance + EPS)
    normalized_input = centered_input * inverse_deviation
    return (normalized_input * scale_gain + shift_bias, normalized_input, inverse_deviation)


def layer_norm_backward(upstream_gradient, normalized_input, inverse_deviation, scale_gain):
    scaled_gradient = upstream_gradient * scale_gain
    incoming_gradient = inverse_deviation * (
        scaled_gradient
        - jnp.mean(scaled_gradient, axis=-1, keepdims=True)
        - normalized_input * jnp.mean(scaled_gradient * normalized_input, axis=-1, keepdims=True)
    )
    return (
        incoming_gradient,
        jnp.sum(upstream_gradient * normalized_input, axis=0),
        jnp.sum(upstream_gradient, axis=0),
    )


def gelu(value):
    return 0.5 * value * (1.0 + jnp.tanh(GELU_C * (value + 0.044715 * value**3)))


def gelu_grad(value):
    tangent = jnp.tanh(GELU_C * (value + 0.044715 * value**3))
    return 0.5 * (1.0 + tangent) + 0.5 * value * (1.0 - tangent * tangent) * GELU_C * (
        1.0 + 3.0 * 0.044715 * value * value
    )


def gather_rows(values):
    return lax.all_gather(values, "tensor", axis=0, tiled=True)


def scatter_rows(values):
    return lax.psum_scatter(values, "tensor", scatter_dimension=0, tiled=True)


def masked_scores(query, key, segs):
    length = segs.shape[0]
    scores = jnp.einsum("qhd,khd->hqk", query, key, preferred_element_type=jnp.float32) * 0.125
    rows = jnp.arange(length)
    allowed = (segs[:, None] == segs[None, :]) & (rows[:, None] >= rows[None, :])
    return jnp.where(allowed[None], scores, -1e30)


def attend(items):
    query, key, value, segs = items
    scores = masked_scores(query, key, segs)
    top = jnp.max(scores, axis=-1, keepdims=True)
    lse = top[..., 0] + jnp.log(jnp.sum(jnp.exp(scores - top), axis=-1))
    weights = jnp.exp(scores - lse[..., None]).astype(jnp.bfloat16)
    output = jnp.einsum("hqk,khd->qhd", weights, value, preferred_element_type=jnp.float32)
    return (output.astype(jnp.bfloat16), lse)


def attend_back(items):
    query, key, value, segs, output, lse, d_out = items
    weights = jnp.exp(masked_scores(query, key, segs) - lse[..., None])
    rounded = weights.astype(jnp.bfloat16)
    d_value = jnp.einsum("hqk,qhd->khd", rounded, d_out, preferred_element_type=jnp.float32)
    d_probs = jnp.einsum("qhd,khd->hqk", d_out, value, preferred_element_type=jnp.float32)
    delta = jnp.transpose(jnp.sum(d_out.astype(jnp.float32) * output.astype(jnp.float32), axis=-1))
    d_scores = (weights * (d_probs - delta[..., None]) * 0.125).astype(jnp.bfloat16)
    d_query = jnp.einsum("hqk,khd->qhd", d_scores, key, preferred_element_type=jnp.float32)
    d_key = jnp.einsum("hqk,qhd->khd", d_scores, query, preferred_element_type=jnp.float32)
    return (d_query.astype(jnp.bfloat16), d_key.astype(jnp.bfloat16), d_value.astype(jnp.bfloat16))


def on_device(
    block_in,
    segment_ids,
    first_norm_gain,
    first_norm_bias,
    qkv_weight,
    qv_bias,
    out_weight,
    out_bias,
    second_norm_gain,
    second_norm_bias,
    fc_weight,
    fc_bias,
    proj_weight,
    proj_bias,
    out_grad,
):
    width = block_in.shape[1]
    local_width = qkv_weight.shape[2]
    heads_dev = local_width // HD
    seq_count = segment_ids.shape[0]
    length = segment_ids.shape[1]
    factor = 1.0 / (seq_count * lax.axis_size("dp"))
    wqkv = qkv_weight.reshape(width, 3 * local_width)
    bias_row = jnp.concatenate([qv_bias[0], jnp.zeros_like(qv_bias[0]), qv_bias[1]])
    layer_input = block_in.astype(jnp.float32)
    first_norm_output, first_normalized_input, first_inverse_deviation = apply_layer_norm(
        layer_input, first_norm_gain, first_norm_bias
    )
    full1 = gather_rows(first_norm_output.astype(jnp.bfloat16))
    qkv = (jnp.dot(full1, wqkv, preferred_element_type=jnp.float32) + bias_row).astype(jnp.bfloat16)
    parts = qkv.reshape(seq_count, length, 3, heads_dev, HD)
    query, key, value = (parts[:, :, 0], parts[:, :, 1], parts[:, :, 2])
    output, lse = lax.map(attend, (query, key, value, segment_ids))
    flat = output.reshape(seq_count * length, local_width)
    middle_state = (
        layer_input
        + scatter_rows(jnp.dot(flat, out_weight, preferred_element_type=jnp.float32))
        + out_bias
    )
    second_norm_output, second_normalized_input, second_inverse_deviation = apply_layer_norm(
        middle_state, second_norm_gain, second_norm_bias
    )
    full2 = gather_rows(second_norm_output.astype(jnp.bfloat16))
    pre = jnp.dot(full2, fc_weight, preferred_element_type=jnp.float32) + fc_bias
    act = gelu(pre).astype(jnp.bfloat16)
    block_out = (
        middle_state
        + scatter_rows(jnp.dot(act, proj_weight, preferred_element_type=jnp.float32))
        + proj_bias
    )
    grad_full = gather_rows(out_grad)
    g_proj_w = jnp.dot(act.T, grad_full, preferred_element_type=jnp.float32) * factor
    d_pre = (
        jnp.dot(grad_full, proj_weight.T, preferred_element_type=jnp.float32) * gelu_grad(pre)
    ).astype(jnp.bfloat16)
    g_fc_w = jnp.dot(full2.T, d_pre, preferred_element_type=jnp.float32) * factor
    g_fc_b = jnp.sum(d_pre.astype(jnp.float32), axis=0) * factor
    second_norm_gradient = scatter_rows(
        jnp.dot(d_pre, fc_weight.T, preferred_element_type=jnp.float32)
    )
    cotf = out_grad.astype(jnp.float32)
    partial_gradient, second_norm_gain_gradient, second_norm_bias_gradient = layer_norm_backward(
        second_norm_gradient, second_normalized_input, second_inverse_deviation, second_norm_gain
    )
    d_mid = cotf + partial_gradient
    g_proj_b = jnp.sum(cotf, axis=0) * factor
    g_out_b = jnp.sum(d_mid, axis=0) * factor
    mid_full = gather_rows(d_mid.astype(jnp.bfloat16))
    g_out_w = jnp.dot(flat.T, mid_full, preferred_element_type=jnp.float32) * factor
    d_o = jnp.dot(mid_full, out_weight.T, preferred_element_type=jnp.float32).astype(jnp.bfloat16)
    d_o = d_o.reshape(seq_count, length, heads_dev, HD)
    d_query, d_key, d_value = lax.map(
        attend_back, (query, key, value, segment_ids, output, lse, d_o)
    )
    d_qkv = jnp.stack([d_query, d_key, d_value], axis=2).reshape(
        seq_count * length, 3 * local_width
    )
    g_qkv_w = (jnp.dot(full1.T, d_qkv, preferred_element_type=jnp.float32) * factor).reshape(
        width, 3, local_width
    )
    query_sum = jnp.sum(d_query.astype(jnp.float32), axis=(0, 1)).reshape(local_width)
    value_sum = jnp.sum(d_value.astype(jnp.float32), axis=(0, 1)).reshape(local_width)
    g_qv_b = jnp.stack([query_sum, value_sum]) * factor
    first_norm_gradient = scatter_rows(jnp.dot(d_qkv, wqkv.T, preferred_element_type=jnp.float32))
    partial_gradient1, first_norm_gain_gradient, first_norm_bias_gradient = layer_norm_backward(
        first_norm_gradient, first_normalized_input, first_inverse_deviation, first_norm_gain
    )
    d_in = d_mid + partial_gradient1
    first_norm_gain_gradient = first_norm_gain_gradient * factor
    first_norm_bias_gradient = first_norm_bias_gradient * factor
    second_norm_gain_gradient = second_norm_gain_gradient * factor
    second_norm_bias_gradient = second_norm_bias_gradient * factor
    g_qkv_w, g_qv_b, g_out_w, g_proj_w, g_fc_w, g_fc_b = lax.psum(
        (g_qkv_w, g_qv_b, g_out_w, g_proj_w, g_fc_w, g_fc_b), "dp"
    )
    (
        first_norm_gain_gradient,
        first_norm_bias_gradient,
        g_out_b,
        second_norm_gain_gradient,
        second_norm_bias_gradient,
        g_proj_b,
    ) = lax.psum(
        (
            first_norm_gain_gradient,
            first_norm_bias_gradient,
            g_out_b,
            second_norm_gain_gradient,
            second_norm_bias_gradient,
            g_proj_b,
        ),
        ("dp", "tensor"),
    )
    return (
        block_out,
        d_in,
        first_norm_gain_gradient,
        first_norm_bias_gradient,
        g_qkv_w,
        g_qv_b,
        g_out_w,
        g_out_b,
        second_norm_gain_gradient,
        second_norm_bias_gradient,
        g_fc_w,
        g_fc_b,
        g_proj_w,
        g_proj_b,
    )


NT = 4
NC = 4
ROWS = 128
ORDER = (0, 3, 1, 2)
BACK = (3, 2, 1, 0)
MESH = pl.DeviceIdType.MESH
F32 = jnp.float32
BF16 = jnp.bfloat16


def mm(a, b):
    return lax.dot_general(a, b, (((1,), (0,)), ((), ())), preferred_element_type=F32)


def mm_nt(a, b):
    return lax.dot_general(a, b, (((1,), (1,)), ((), ())), preferred_element_type=F32)


def mm_tn(a, b):
    return lax.dot_general(a, b, (((0,), (0,)), ((), ())), preferred_element_type=F32)


def norm_stats(values):
    centered = values - jnp.mean(values, axis=-1, keepdims=True)
    rstd = lax.rsqrt(jnp.mean(centered * centered, axis=-1, keepdims=True) + EPS)
    return centered * rstd, rstd


def norm_back(cot, xhat, rstd, gain):
    e = cot * gain
    return rstd * (
        e
        - jnp.mean(e, axis=-1, keepdims=True)
        - xhat * jnp.mean(e * xhat, axis=-1, keepdims=True)
    )


def layer_kernel(
    x_ref, g_ref, seg_row, gain1, shift1, wqkv, qvb, wout, bout, gain2, shift2, wfc, bfc, wproj, bproj,
    bo_out, din_out, grad_out, vec_out, qv_out,
    xfull, gfull, wfull, n1, qh, kh, vh, pscr, ofull, mid, n2, act, dpre,
    bo_send, dn2_send, dn1_send, bo_recv, dn2_recv, dn1_recv, dmid, dmid_own,
    dkacc, dvacc, dqkv, gl, d2d, hsum, rs, vsend, vbuf, wsend, wbuf,
    x_s, x_r, g_s, g_r, w1_s, w1_r, w2_s, w2_r, loc_s, o_s, o_r, n2_s, n2_r, n1_s, n1_r,
    b_s, b_r, m_s, m_r, d1_s, d1_r, rs_s, rs_r, ag_s, ag_r, d2_s, d2_r, va_s, va_r, vb_s, vb_r,
):
    d = lax.axis_index("dp")
    t = lax.axis_index("tensor")
    chip = d // 2
    core = d % 2

    def at_t(o):
        return (d, lax.rem(t + o, NT))

    def at_d(o):
        return (lax.rem(d + o, 8), t)

    def at_chip(o):
        return (lax.rem(chip + o, NC) * 2 + core, t)

    sibling = (chip * 2 + 1 - core, t)

    barrier = pltpu.get_barrier_semaphore()
    for o in range(1, NT):
        pl.semaphore_signal(barrier, inc=1, device_id=at_t(o), device_id_type=MESH)
    for o in range(1, 8):
        pl.semaphore_signal(barrier, inc=1, device_id=at_d(o), device_id_type=MESH)
    pl.semaphore_wait(barrier, NT - 1 + 7)

    pending = []
    ln1 = (gain1[...][None], shift1[...][None])
    ln2 = (gain2[...][None], shift2[...][None], bout[...][None])
    bqkv = jnp.concatenate([qvb[0:1, :], jnp.zeros((1, 192), F32), qvb[1:2, :]], axis=1)
    bfc_row = bfc[...][None]
    seg_col = jnp.transpose(jnp.broadcast_to(seg_row[...].astype(F32), (ROWS, 512)))[:, 0:1]
    seg_line = seg_row[...].astype(F32)

    def rcopy(src, dst, ss, rsem, dev):
        return pltpu.make_async_remote_copy(
            src_ref=src, dst_ref=dst, send_sem=ss, recv_sem=rsem, device_id=dev, device_id_type=MESH
        )

    def go(*args):
        c = rcopy(*args)
        c.start()
        pending.append(c)
        return c

    def rows_of(j):
        return pl.ds(pl.multiple_of(j * ROWS, ROWS), ROWS)

    def hop_send(k, ref, ss, rsem, r=None):
        def go_to(cond, slot, side, to):
            @pl.when(cond)
            def _():
                b = ref.at[slot] if r is None else ref.at[slot, r]
                rcopy(b, b, ss.at[side, k], rsem.at[side, k], (d, to)).start()

        go_to((t < NT - 1) & (t >= k), t - k, 0, t + 1)
        go_to((t > 0) & (t + k < NT), t + k, 1, t - 1)

    def hop_wait(k, ref, ss, rsem, r=None):
        b = ref.at[0] if r is None else ref.at[0, r]

        @pl.when(t >= k + 1)
        def _():
            rcopy(b, b, ss.at[0, k], rsem.at[0, k], at_t(1)).wait_recv()

        @pl.when(t + k + 1 < NT)
        def _():
            rcopy(b, b, ss.at[1, k], rsem.at[1, k], at_t(1)).wait_recv()

    def hop_sent(ref, ss, rsem, r=None):
        b = ref.at[0] if r is None else ref.at[0, r]
        for k in range(NT - 1):

            @pl.when((t < NT - 1) & (t >= k))
            def _():
                rcopy(b, b, ss.at[0, k], rsem.at[0, k], at_t(1)).wait_send()

            @pl.when((t > 0) & (t + k < NT))
            def _():
                rcopy(b, b, ss.at[1, k], rsem.at[1, k], at_t(1)).wait_send()

    def sum_hop(k, j, send, recv, ss, rsem):
        for side, here, to in ((0, k, 1), (1, NT - 1 - k, -1)):
            if (here < j) if side == 0 else (here > j):

                @pl.when(t == here)
                def _():
                    c = rcopy(
                        send.at[j], recv.at[side, j], ss.at[j], rsem.at[side, j], (d, here + to)
                    )
                    if k:
                        c.wait_recv()
                        send[j] = (send[j].astype(F32) + recv[side, j].astype(F32)).astype(BF16)
                    c.start()

    def sum_steps(i, order, *bufs):
        for k in range(NT - 1):
            if 0 <= i - k < NT:
                sum_hop(k, order[i - k], *bufs)

    def sum_ends(recv):
        @pl.when(t == 0)
        def _():
            recv[0, 0] = jnp.zeros((ROWS, 768), BF16)

        @pl.when(t == NT - 1)
        def _():
            recv[1, NT - 1] = jnp.zeros((ROWS, 768), BF16)

    def gathered(send, recv, ss, rsem):
        @pl.when(t > 0)
        def _():
            rcopy(send.at[t], recv.at[0, t], ss.at[t], rsem.at[0, t], at_t(1)).wait_recv()

        @pl.when(t < NT - 1)
        def _():
            rcopy(send.at[t], recv.at[1, t], ss.at[t], rsem.at[1, t], at_t(1)).wait_recv()

        return send[t].astype(F32) + recv[0, t].astype(F32) + recv[1, t].astype(F32)

    xfull[t] = x_ref[...]
    gfull[t] = g_ref[...]
    hop_send(0, xfull, x_s, x_r)
    cols = pl.ds(pl.multiple_of(core * 384, 128), 384)
    wsrc = wout.at[pl.ds(pl.multiple_of(chip * 48, 16), 48), cols]
    own_w = pltpu.make_async_copy(wsrc, wfull.at[t, chip, :, cols], loc_s)
    own_w.start()
    cw1 = [
        go(wsrc, wfull.at[t, chip, :, cols], w1_s.at[o], w1_r.at[o], at_t(o))
        for o in range(1, NT)
    ]
    for buf in (bo_recv, dn2_recv, dn1_recv):
        sum_ends(buf)

    def project(s):
        xhat, _ = norm_stats(xfull[s].astype(F32))
        nb = (xhat * ln1[0] + ln1[1]).astype(BF16)
        n1[rows_of(s), :] = nb
        qkv = (mm_nt(nb, wqkv[...]) + bqkv).astype(BF16)
        for h in range(3):
            qh[h, rows_of(s), :] = qkv[:, h * HD : h * HD + HD]
            kh[h, rows_of(s), :] = qkv[:, 192 + h * HD : 192 + h * HD + HD]
            vh[h, rows_of(s), :] = qkv[:, 384 + h * HD : 384 + h * HD + HD]

    project(t)
    hop_wait(0, xfull, x_s, x_r)
    hop_send(1, xfull, x_s, x_r)
    near = t + 1 - 2 * lax.rem(t, 2)
    project(near)
    hop_wait(1, xfull, x_s, x_r)
    hop_send(2, xfull, x_s, x_r)
    hop_send(0, gfull, g_s, g_r)
    own_w.wait()
    for c in cw1:
        c.wait_recv()
    wpart = wfull.at[:, chip, :, cols]
    hop_wait(2, xfull, x_s, x_r)
    far = lax.rem(t + 2, NT)
    project(far)
    project(far + 1 - 2 * lax.rem(far, 2))
    cw2 = [go(wpart, wpart, w2_s.at[o], w2_r.at[o], at_d(o)) for o in range(1, 8)]

    def o_hops(i):
        for k in range(NT):
            if 0 <= i - k < NT:
                j = ORDER[i - k]
                args = (ofull, o_s.at[j], o_r.at[j], slice(j * ROWS, (j + 1) * ROWS))
                if k:
                    hop_wait(k - 1, *args)
                if k < NT - 1:
                    hop_send(k, *args)

    for i, j in enumerate(ORDER):
        r = slice(j * ROWS, (j + 1) * ROWS)
        n = (j + 1) * ROWS
        qi = j * ROWS + lax.broadcasted_iota(jnp.int32, (ROWS, n), 0)
        ki = lax.broadcasted_iota(jnp.int32, (ROWS, n), 1)
        allowed = (seg_col[r, :] == seg_line[:, :n]) & (qi >= ki)
        outs = []
        for h in range(3):
            sc = jnp.where(allowed, mm_nt(qh[h, r, :], kh[h, :n, :]) * 0.125, -1e30)
            e = jnp.exp(sc - jnp.max(sc, axis=-1, keepdims=True))
            p = e * (1.0 / jnp.sum(e, axis=-1, keepdims=True))
            pscr[h, r, :n] = p
            outs.append(mm(p.astype(BF16), vh[h, :n, :]))
        ofull[t, r, :] = jnp.concatenate(outs, axis=1).astype(BF16)
        o_hops(i)
        if i == 0:
            hop_wait(0, gfull, g_s, g_r)
            hop_send(1, gfull, g_s, g_r)
        if i == 2:
            hop_wait(1, gfull, g_s, g_r)
            hop_send(2, gfull, g_s, g_r)

    for c in cw2:
        c.wait_recv()
    hop_wait(2, gfull, g_s, g_r)

    dn2_sum = (dn2_send, dn2_recv, n2_s, n2_r)
    bo_sum = (bo_send, bo_recv, b_s, b_r)
    dn1_sum = (dn1_send, dn1_recv, n1_s, n1_r)
    for i, j in enumerate(ORDER):
        r = slice(j * ROWS, (j + 1) * ROWS)
        if i:
            o_hops(i + 3)
        m = xfull[j].astype(F32) + ln2[2]
        for s in range(NT):
            m = m + mm(ofull[s, r, :], wfull[s].reshape(192, 768))
        mid[r, :] = m
        xhat, _ = norm_stats(m)
        nb = (xhat * ln2[0] + ln2[1]).astype(BF16)
        n2[r, :] = nb
        pre = mm(nb, wfc[...]) + bfc_row
        sq = pre * pre
        tangent = jnp.tanh(GELU_C * (pre + 0.044715 * (sq * pre)))
        slope = 0.5 * (1.0 + tangent) + 0.5 * pre * (1.0 - tangent * tangent) * GELU_C * (
            1.0 + 3.0 * 0.044715 * sq
        )
        ab = (0.5 * pre * (1.0 + tangent)).astype(BF16)
        act[r, :] = ab
        dp = (mm_nt(gfull[j], wproj[...]) * slope).astype(BF16)
        dpre[r, :] = dp
        dn2_send[j] = mm_nt(dp, wfc[...]).astype(BF16)

        sum_steps(i, ORDER, *dn2_sum)
        bo_send[j] = mm(ab, wproj[...]).astype(BF16)

    def stage1(i):
        half = pl.ds(pl.multiple_of((1 - core) * 384, 128), 384)
        return go(gl.at[i, half], d2d.at[i], d1_s.at[i], d1_r.at[i], sibling)

    def stage2(i, c):
        c.wait_recv()
        half = pl.ds(pl.multiple_of(core * 384, 128), 384)
        hsum[i] = (gl[i, half, :].astype(F32) + d2d[i].astype(F32)).astype(BF16)
        out = []
        for o in range(1, NC):
            to = pl.ds(pl.multiple_of(lax.rem(chip + o, NC) * 96, 32), 96)
            out.append(go(hsum.at[i, to], rs.at[i, o], rs_s.at[i, o], rs_r.at[i, o], at_chip(o)))
        return out

    def stage3(i, cs):
        own = pl.ds(pl.multiple_of(chip * 96, 32), 96)
        total = hsum[i, own, :].astype(F32)
        for o in range(1, NC):
            cs[o - 1].wait_recv()
            total = total + rs[i, o].astype(F32)
        at = pl.ds(pl.multiple_of(core * 384 + chip * 96, 32), 96)
        grad_out[i, at, :] = total.astype(BF16)
        blk = grad_out.at[i, at]
        return [
            go(blk, blk, ag_s.at[i, o], ag_r.at[i, o], at_chip(o)) for o in range(1, NC)
        ]

    def stage4(i, cs):
        for c in cs:
            c.wait_recv()
        half = grad_out.at[i, pl.ds(pl.multiple_of(core * 384, 128), 384)]
        return go(half, half, d2_s.at[i], d2_r.at[i], sibling)

    sum_steps(4, ORDER, *dn2_sum)
    gmat = gfull[...].reshape(NT * ROWS, 768)
    gl[0] = mm_tn(act[...], gmat).astype(BF16)
    c1a = stage1(0)
    sum_steps(5, ORDER, *dn2_sum)

    own_rows = rows_of(t)
    gown = g_ref[...].astype(F32)
    dn2 = gathered(*dn2_sum)
    xhat, rstd = norm_stats(mid[own_rows, :])
    dm = gown + norm_back(dn2, xhat, rstd, ln2[0])
    dmid_own[...] = dm
    dmid[t] = dm.astype(BF16)
    hop_send(0, dmid, m_s, m_r)
    vsend[2:3, :] = jnp.sum(dm, axis=0, keepdims=True)
    vsend[3:4, :] = jnp.sum(dn2 * xhat, axis=0, keepdims=True)
    vsend[4:5, :] = jnp.sum(dn2, axis=0, keepdims=True)
    vsend[5:6, :] = jnp.sum(gown, axis=0, keepdims=True)
    vsend[6:7, :] = jnp.sum(dpre[...].astype(F32), axis=0, keepdims=True)
    hop_wait(0, dmid, m_s, m_r)
    hop_send(1, dmid, m_s, m_r)
    gl[1] = mm_tn(n2[...], dpre[...]).astype(BF16)
    c1b = stage1(1)
    c2a = stage2(0, c1a)
    hop_wait(1, dmid, m_s, m_r)
    hop_send(2, dmid, m_s, m_r)
    c2b = stage2(1, c1b)
    hop_wait(2, dmid, m_s, m_r)
    sum_steps(0, ORDER, *bo_sum)

    dkacc[...] = jnp.zeros_like(dkacc)
    dvacc[...] = jnp.zeros_like(dvacc)
    for i, j in enumerate(BACK):
        r = slice(j * ROWS, (j + 1) * ROWS)
        n = (j + 1) * ROWS

        do = mm_nt(dmid[j], wout[...]).astype(BF16)
        ob = ofull[t, r, :].astype(F32) * do.astype(F32)
        dq = []
        for h in range(3):
            hs = slice(h * HD, h * HD + HD)
            doh = do[:, hs]
            p = pscr[h, r, :n]
            dvacc[h, :n, :] += mm_tn(p.astype(BF16), doh)
            delta = jnp.sum(ob[:, hs], axis=-1, keepdims=True)
            ds = (p * (mm_nt(doh, vh[h, :n, :]) - delta) * 0.125).astype(BF16)
            dq.append(mm(ds, kh[h, :n, :]))
            dkacc[h, :n, :] += mm_tn(ds, qh[h, r, :])
        parts = dq + [dkacc[h, r, :] for h in range(3)] + [dvacc[h, r, :] for h in range(3)]
        dqkv[r, :] = jnp.concatenate(parts, axis=1).astype(BF16)
        dn1_send[j] = mm(dqkv[r, :], wqkv[...]).astype(BF16)
        sum_steps(i, BACK, *dn1_sum)
        if i < 3:
            sum_steps(i + 1, ORDER, *bo_sum)

        if j == 1:
            c3a = stage3(0, c2a)
            c3b = stage3(1, c2b)

    gl[2, 0:576, :] = mm_tn(dqkv[...], n1[...]).astype(BF16)
    gl[2, 576:768, :] = mm_tn(ofull[t], dmid[...].reshape(NT * ROWS, 768)).astype(BF16)
    c1c = stage1(2)
    sum_steps(4, BACK, *dn1_sum)
    dsum = jnp.sum(dqkv[...].astype(F32), axis=0, keepdims=True)
    vsend[7:8, :] = jnp.concatenate([dsum, jnp.zeros((1, 192), F32)], axis=1)
    c4a = stage4(0, c3a)
    c4b = stage4(1, c3b)
    c2c = stage2(2, c1c)
    sum_steps(5, BACK, *dn1_sum)
    sum_steps(4, ORDER, *bo_sum)
    sum_steps(5, ORDER, *bo_sum)
    bo = gathered(*bo_sum)
    bo_out[...] = mid[own_rows, :] + bo + bproj[...][None]
    dn1 = gathered(*dn1_sum)
    xhat, rstd = norm_stats(x_ref[...].astype(F32))
    din_out[...] = dmid_own[...] + norm_back(dn1, xhat, rstd, ln1[0])
    vsend[0:1, :] = jnp.sum(dn1 * xhat, axis=0, keepdims=True)
    vsend[1:2, :] = jnp.sum(dn1, axis=0, keepdims=True)
    cva = [go(vsend, vbuf.at[t], va_s.at[o], va_r.at[o], at_t(o)) for o in range(1, NT)]
    vbuf[t] = vsend[...]
    c3c = stage3(2, c2c)
    for c in cva:
        c.wait_recv()
    wsend[...] = ((vbuf[0] + vbuf[1]) + vbuf[2]) + vbuf[3]
    wsend[6:8, :] = vsend[6:8, :]
    cvb = [go(wsend, wbuf.at[d], vb_s.at[o], vb_r.at[o], at_d(o)) for o in range(1, 8)]
    wbuf[d] = wsend[...]
    c4c = stage4(2, c3c)
    for c in cvb:
        c.wait_recv()
    total = wbuf[0]
    for s in range(1, 8):
        total = total + wbuf[s]
    total = total * 0.125
    vec_out[...] = total
    qv_out[0:1, :] = total[7:8, 0:192]
    qv_out[1:2, :] = total[7:8, 384:576]
    c4a.wait_recv()
    c4b.wait_recv()
    c4c.wait_recv()

    for c in pending:
        c.wait_send()
    for args in ((xfull, x_s, x_r), (gfull, g_s, g_r), (dmid, m_s, m_r)):
        hop_sent(*args)
    for j in range(NT):
        hop_sent(ofull, o_s.at[j], o_r.at[j], slice(j * ROWS, (j + 1) * ROWS))

        @pl.when(t != j)
        def _():
            for send, recv, ss, rsem in (dn2_sum, bo_sum, dn1_sum):
                rcopy(send.at[j], recv.at[0, j], ss.at[j], rsem.at[0, j], at_t(1)).wait_send()


def on_device_fused(
    block_in, segment_ids, first_norm_gain, first_norm_bias, qkv_weight, qv_bias, out_weight,
    out_bias, second_norm_gain, second_norm_bias, fc_weight, fc_bias, proj_weight, proj_bias,
    out_grad,
):
    wqkv = jnp.transpose(qkv_weight, (1, 2, 0)).reshape(576, 768)
    full = lambda dt: pltpu.VMEM((NT, ROWS, 768), dt)
    head = lambda dt: pltpu.VMEM((3, 512, HD), dt)
    tall = lambda n, dt: pltpu.VMEM((512, n), dt)
    dma = lambda *s: pltpu.SemaphoreType.DMA(s)
    pair = pltpu.VMEM((2, NT, ROWS, 768), BF16)
    hops = (2, NT - 1)
    scratch = [
        full(BF16), full(BF16), pltpu.VMEM((NT, NC, 48, 768), BF16), tall(768, BF16),
        head(BF16), head(BF16), head(BF16), pltpu.VMEM((3, 512, 512), F32),
        pltpu.VMEM((NT, 512, 192), BF16), tall(768, F32), tall(768, BF16), tall(768, BF16),
        tall(768, BF16),
        full(BF16), full(BF16), full(BF16), pair, pair, pair, full(BF16),
        pltpu.VMEM((ROWS, 768), F32),
        head(F32), head(F32), tall(576, BF16),
        pltpu.VMEM((3, 768, 768), BF16), pltpu.VMEM((3, 384, 768), BF16),
        pltpu.VMEM((3, 384, 768), BF16), pltpu.VMEM((3, NC, 96, 768), BF16),
        pltpu.VMEM((8, 768), F32), pltpu.VMEM((NT, 8, 768), F32),
        pltpu.VMEM((8, 768), F32), pltpu.VMEM((8, 8, 768), F32),
        dma(*hops), dma(*hops), dma(*hops), dma(*hops), dma(4), dma(4), dma(8), dma(8), pltpu.SemaphoreType.DMA,
        dma(4, *hops), dma(4, *hops), dma(4), dma(2, 4), dma(4), dma(2, 4), dma(4), dma(2, 4),
        dma(*hops), dma(*hops),
        dma(3), dma(3), dma(3, 4), dma(3, 4), dma(3, 4), dma(3, 4), dma(3), dma(3),
        dma(4), dma(4), dma(8), dma(8),
    ]
    vm = pl.BlockSpec(memory_space=pltpu.VMEM)
    block_out, d_in, grads, vecs, qv = pl.pallas_call(
        layer_kernel,
        out_shape=(
            jax.ShapeDtypeStruct((ROWS, 768), F32),
            jax.ShapeDtypeStruct((ROWS, 768), F32),
            jax.ShapeDtypeStruct((3, 768, 768), BF16),
            jax.ShapeDtypeStruct((8, 768), F32),
            jax.ShapeDtypeStruct((2, 192), F32),
        ),
        in_specs=[vm] * 15,
        out_specs=[vm] * 5,
        scratch_shapes=scratch,
        compiler_params=pltpu.CompilerParams(
            collective_id=0, has_side_effects=True, vmem_limit_bytes=60 * 1024 * 1024
        ),
        cost_estimate=pl.CostEstimate(
            flops=8_000_000_000, bytes_accessed=12_000_000, transcendentals=2_000_000
        ),
    )(
        block_in, out_grad, segment_ids, first_norm_gain, first_norm_bias, wqkv, qv_bias,
        out_weight, out_bias, second_norm_gain, second_norm_bias, fc_weight, fc_bias, proj_weight,
        proj_bias,
    )
    scaled = lambda a: a.astype(F32) * 0.125
    return (
        block_out,
        d_in,
        vecs[0],
        vecs[1],
        jnp.transpose(scaled(grads[2, :576]).reshape(3, 192, 768), (2, 0, 1)),
        qv,
        scaled(grads[2, 576:]),
        vecs[2],
        vecs[3],
        vecs[4],
        scaled(grads[1]),
        vecs[6],
        scaled(grads[0]),
        vecs[5],
    )


def solution(mesh):
    fits = mesh.shape["dp"] == 8 and mesh.shape["tensor"] == 4
    return jax.shard_map(
        on_device_fused if fits else on_device,
        mesh=mesh,
        in_specs=(
            P(("dp", "tensor"), None),
            P("dp", None),
            P(),
            P(),
            P(None, None, "tensor"),
            P(None, "tensor"),
            P("tensor", None),
            P(),
            P(),
            P(),
            P(None, "tensor"),
            P("tensor"),
            P("tensor", None),
            P(),
            P(("dp", "tensor"), None),
        ),
        out_specs=(
            P(("dp", "tensor"), None),
            P(("dp", "tensor"), None),
            P(),
            P(),
            P(None, None, "tensor"),
            P(None, "tensor"),
            P("tensor", None),
            P(),
            P(),
            P(),
            P(None, "tensor"),
            P("tensor"),
            P("tensor", None),
            P(),
        ),
        check_vma=False,
    )
```
